256 devices in a mesh: rows: 32 (over x, y, z_lo), chan: 8 (over z_hi, core).
Axes of the slice: x: 4, y: 4, z: 8 (z_hi: 4, z_lo: 2; z = z_hi * 2 + z_lo), core: 2. Of those that a mesh axis runs over, the one named last changes fastest.
Arguments:
- frame_adjoint: bfloat16 [32, 192, 32, 128], P('rows', 'chan'), may hold values from -6 to 6
- frame_slot: int32 [32], replicated, may hold values from 0 to 31, each once
- inputs: bfloat16 [32, 192, 32, 128], P(None, 'chan', 'rows')
- gain: float32 [192], P('chan'), may hold values from 0.1 to 1.9
- weight: bfloat16 [27, 192, 192], P(None, 'chan'), may hold values from -0.078125 to 0.078125
Outputs:
- input_adjoint: bfloat16 [32, 192, 32, 128], P(None, 'chan', 'rows')
- weight_adjoint: float32 [27, 192, 192], P(None, 'chan')
The draws below stay inside these ranges and needn't reach their ends.
Inputs may be any that keep to these rules, and one draw needn't show every extreme that they name: `frame_slot`: each frame appears in exactly one slot.
All inputs are finite; a program needn't handle non-finite values.
Results may differ from the reference program's by a relative error of at most 0.003.
Values may be sent and summed in bfloat16 or wider, within the bound.
A program may use at most 128 MiB of HBM per device.

```python
import math
import jax
import jax.numpy as jnp
from jax import lax

CHANNELS = 192
TAPS = 27
WIDTH = 128
FRAMES = 32
HEIGHT = 32


def draw_inputs(key, part):
    key = jax.random.fold_in(key, 11)
    first, second, third = jax.random.split(key, 3)
    shape = (FRAMES, CHANNELS, HEIGHT, WIDTH)
    base = jax.random.normal(first, shape, jnp.float32)
    rising = jnp.exp(math.log(3.0) * jnp.arange(CHANNELS, dtype=jnp.float32) / CHANNELS)
    spread = jnp.exp(jax.random.uniform(second, (CHANNELS,), jnp.float32, 0.0, math.log(10.0)))
    pixel = jnp.exp(jax.random.uniform(third, (FRAMES, 1, HEIGHT, WIDTH), jnp.float32, 0.0, math.log(10.0)))
    values = base * (rising * spread)[None, :, None, None] * pixel * 0.3
    return values.astype(jnp.bfloat16)


def block_scale(key, dims, cuts, low, top_value):
    loudness = 1.0
    for dim, shards_of in cuts:
        heights = jax.random.uniform(jax.random.fold_in(jax.random.fold_in(key, 6), dim), (shards_of,), jnp.float32, low / len(cuts), top_value / len(cuts))
        loudness = loudness * jnp.repeat(jnp.exp(heights), dims[dim] // shards_of).reshape((-1,) + (1,) * (len(dims) - 1 - dim))
    return loudness


def gaussian(own_key, extent, scale, most, shards=(), kind=jnp.bfloat16):
    factor_of = block_scale(own_key, extent, shards, -0.22, 0.18) if shards else 1.0
    values = jax.random.normal(own_key, extent, jnp.float32) * scale * factor_of
    return jnp.minimum(jnp.maximum(values, -most), most).astype(kind)


def setup_inputs(seed: int = 0) -> dict:
    key_of = jax.random.split(jax.random.key(seed), 6)
    return {
        "frame_adjoint": gaussian(key_of[0], (FRAMES, CHANNELS, HEIGHT, WIDTH), 1.0, 6.0, ((0, 32), (1, 8))),
        "frame_slot": jax.random.permutation(key_of[1], FRAMES).astype(jnp.int32),
        "inputs": draw_inputs(jax.random.fold_in(key_of[5], 71), 0),
        "gain": jnp.clip(1.0 + 0.18 * jax.random.normal(key_of[3], (CHANNELS,), jnp.float32), 0.1, 1.9),
        "weight": gaussian(key_of[4], (TAPS, CHANNELS, CHANNELS), (TAPS * CHANNELS) ** -0.5, 0.078125, ((1, 8),)),
    }


epsilon = 1e-06

def reference(frame_adjoint, frame_slot, inputs, gain, weight):
    onehot = (frame_slot[None, :] == jnp.arange(FRAMES, dtype=jnp.int32)[:, None]).astype(jnp.float32)
    adjoint = jnp.einsum('tj,jcrw->tcrw', onehot, frame_adjoint.astype(jnp.float32))
    values = inputs.astype(jnp.float32)
    scale = lax.rsqrt(lax.optimization_barrier(jnp.sum(values * values, axis=1)) / CHANNELS + epsilon)[:, None]
    normed = values * scale * gain[None, :, None, None]
    sigma = jax.nn.sigmoid(normed)
    hidden = (normed * sigma).astype(jnp.bfloat16).astype(jnp.float32)
    hidden_pad = jnp.pad(hidden, ((2, 0), (0, 0), (1, 1), (1, 1)))
    adjoint_pad = jnp.pad(adjoint, ((0, 2), (0, 0), (1, 1), (1, 1)))
    kernel = weight.astype(jnp.float32)
    hidden_adjoint = jnp.zeros(values.shape, jnp.float32)
    grad_list = []
    for frame_off in range(3):
        for row_off in range(3):
            for col_off in range(3):
                index = frame_off * 9 + row_off * 3 + col_off
                window = adjoint_pad[2 - frame_off:2 - frame_off + FRAMES, :, 2 - row_off:2 - row_off + HEIGHT, 2 - col_off:2 - col_off + WIDTH]
                hidden_adjoint = hidden_adjoint + jnp.einsum('forw,oc->fcrw', window, kernel[index])
                source = hidden_pad[frame_off:frame_off + FRAMES, :, row_off:row_off + HEIGHT, col_off:col_off + WIDTH]
                grad_list.append(jnp.einsum('forw,fcrw->oc', adjoint, source))
    weight_adjoint = jnp.stack(grad_list) * float(FRAMES * HEIGHT * WIDTH) ** (-0.5)
    normed_adjoint = hidden_adjoint * sigma * (1.0 + normed * (1.0 - sigma)) * gain[None, :, None, None]
    projection = lax.optimization_barrier(jnp.sum(normed_adjoint * values, axis=1))[:, None]
    input_adjoint = scale * normed_adjoint - values * scale * scale * scale * projection / CHANNELS
    return (input_adjoint.astype(jnp.bfloat16), weight_adjoint)
```

```python
import jax
import jax.numpy as jnp
from jax import lax
from jax.experimental import pallas as pl
from jax.experimental.pallas import tpu as pltpu
from jax.sharding import PartitionSpec as P

CHANNELS = 192
GROUP = 24
WIDTH = 128
ROWS = 32
CHAN = 8
HALF = 4
TAPS = 27
WINDOW = 80
SLAB = 72
KBLOCK = 224
EPSILON = 1e-06
MESH = pl.DeviceIdType.MESH
VMEM_LIMIT = 56 * 1024 * 1024


def greet(rows_me, chan_me):
    barrier = pltpu.get_barrier_semaphore()

    def rows_step(d, carry):
        pl.semaphore_signal(
            barrier, inc=1, device_id={"rows": lax.rem(rows_me + d, ROWS)}, device_id_type=MESH
        )
        return carry

    def chan_step(d, carry):
        pl.semaphore_signal(
            barrier, inc=1, device_id={"chan": lax.rem(chan_me + d, CHAN)}, device_id_type=MESH
        )
        return carry

    lax.fori_loop(1, ROWS, rows_step, 0)
    lax.fori_loop(1, CHAN, chan_step, 0)
    pl.semaphore_wait(barrier, ROWS - 1 + CHAN - 1)


def send(src, dst, send_sem, recv_sem, device):
    pltpu.make_async_remote_copy(
        src_ref=src,
        dst_ref=dst,
        send_sem=send_sem,
        recv_sem=recv_sem,
        device_id=device,
        device_id_type=MESH,
    ).start()


def drain(ref, sem):
    pltpu.make_async_copy(ref, ref, sem).wait()


def exchange_kernel(
    inverse, win, x, gain, w, adj_out, x_out, gain_out, w_out, recv, ordered, sems, local
):
    r = lax.axis_index("rows")
    c = lax.axis_index("chan")
    h = c // 2
    win_s, win_r, x_s, x_r, g_s, g_r, w_s, w_r, a_s, a_r = [sems.at[i] for i in range(10)]

    own_win = pltpu.make_async_copy(win.at[r], recv.at[r], local.at[0])
    own_win.start()
    greet(r, c)

    def win_step(d, carry):
        target = lax.rem(r + d, ROWS)
        send(win.at[target], recv.at[r], win_s, win_r, {"rows": target})
        return carry

    lax.fori_loop(1, ROWS, win_step, 0)

    def x_step(d, carry):
        target = lax.rem(c + d, CHAN)
        begin = pl.multiple_of((target // 2) * 192, 64)
        send(x.at[pl.ds(begin, 192)], x_out.at[c], x_s, x_r, {"chan": target})
        send(gain, gain_out.at[c], g_s, g_r, {"chan": target})
        return carry

    lax.fori_loop(1, CHAN, x_step, 0)

    def w_step(d, carry):
        target = lax.rem(c + 2 * d, CHAN)
        send(w, w_out.at[h], w_s, w_r, {"chan": target})
        return carry

    lax.fori_loop(1, HALF, w_step, 0)
    begin = pl.multiple_of(h * 192, 64)
    own_x = pltpu.make_async_copy(x.at[pl.ds(begin, 192)], x_out.at[c], local.at[1])
    own_gain = pltpu.make_async_copy(gain, gain_out.at[c], local.at[2])
    own_w = pltpu.make_async_copy(w, w_out.at[h], local.at[3])
    own_x.start()
    own_gain.start()
    own_w.start()

    ordered[pl.ds(32 * SLAB, 2 * SLAB), :] = jnp.zeros((2 * SLAB, WIDTH), jnp.bfloat16)
    own_win.wait()
    drain(recv.at[pl.ds(0, ROWS - 1)], win_r)

    def order_step(p, carry):
        low = recv[inverse[2 * p]].astype(jnp.float32)[:SLAB]
        high = recv[inverse[2 * p + 1]].astype(jnp.float32)[:SLAB]
        both = jnp.concatenate([low, high], axis=0).astype(jnp.bfloat16)
        ordered[pl.ds(pl.multiple_of(p * 2 * SLAB, 2 * SLAB), 2 * SLAB), :] = both
        return carry

    lax.fori_loop(0, ROWS // 2, order_step, 0)

    def a_step(d, carry):
        target = lax.rem(c + 2 * d, CHAN)
        start = pl.multiple_of((target // 2) * (8 * SLAB), 64)
        send(ordered.at[pl.ds(start, 10 * SLAB)], adj_out.at[h], a_s, a_r, {"chan": target})
        return carry

    lax.fori_loop(1, HALF, a_step, 0)
    start = pl.multiple_of(h * (8 * SLAB), 64)
    own_adj = pltpu.make_async_copy(
        ordered.at[pl.ds(start, 10 * SLAB)], adj_out.at[h], local.at[4]
    )
    own_adj.start()
    own_x.wait()
    own_gain.wait()
    own_w.wait()
    own_adj.wait()
    drain(win.at[pl.ds(0, ROWS - 1)], win_s)
    drain(x_out.at[pl.ds(0, CHAN - 1)], x_s)
    drain(gain_out.at[pl.ds(0, CHAN - 1)], g_s)
    drain(w_out.at[pl.ds(0, HALF - 1)], w_s)
    drain(adj_out.at[pl.ds(0, HALF - 1)], a_s)
    drain(x_out.at[pl.ds(0, CHAN - 1)], x_r)
    drain(gain_out.at[pl.ds(0, CHAN - 1)], g_r)
    drain(w_out.at[pl.ds(0, HALF - 1)], w_r)
    drain(adj_out.at[pl.ds(0, HALF - 1)], a_r)


def exchange(inverse, win, x, gain, w):
    anywhere = pl.BlockSpec(memory_space=pl.ANY)
    return pl.pallas_call(
        exchange_kernel,
        out_shape=(
            jax.ShapeDtypeStruct((HALF, 10 * SLAB, WIDTH), jnp.bfloat16),
            jax.ShapeDtypeStruct((CHAN, 8 * GROUP, WIDTH), jnp.bfloat16),
            jax.ShapeDtypeStruct((CHAN, GROUP, WIDTH), jnp.float32),
            jax.ShapeDtypeStruct((HALF, 3 * KBLOCK, CHANNELS), jnp.bfloat16),
        ),
        in_specs=[pl.BlockSpec(memory_space=pltpu.SMEM)] + [anywhere] * 4,
        out_specs=(anywhere,) * 4,
        scratch_shapes=[
            pltpu.VMEM((ROWS, WINDOW, WIDTH), jnp.bfloat16),
            pltpu.VMEM((34 * SLAB, WIDTH), jnp.bfloat16),
            pltpu.SemaphoreType.DMA((10,)),
            pltpu.SemaphoreType.DMA((5,)),
        ],
        compiler_params=pltpu.CompilerParams(
            collective_id=0, has_side_effects=True, vmem_limit_bytes=VMEM_LIMIT
        ),
    )(inverse, win, x, gain, w)


def norm_of(values, gain):
    squares = jnp.sum(values * values, axis=0, keepdims=True)
    scale = lax.rsqrt(squares / CHANNELS + EPSILON)
    return scale, values * scale * gain


def sigmoid(v):
    return 1.0 / (1.0 + jnp.exp(-v))


def compute_kernel(adj, x, gain, w, grad_out, part_out, stack, hidden):
    gains = gain[...]
    for f in range(8):
        values = jnp.concatenate(
            [x[g].astype(jnp.float32)[GROUP * f : GROUP * f + GROUP] for g in range(CHAN)], axis=0
        )
        _, normed = norm_of(values, gains)
        hidden[:, WIDTH * f : WIDTH * (f + 1)] = (normed * sigmoid(normed)).astype(jnp.bfloat16)

    lane = lax.broadcasted_iota(jnp.int32, (10 * SLAB, WIDTH), 1)

    def stack_step(g, carry):
        middle = adj[g].astype(jnp.float32)
        ahead = jnp.where(lane == WIDTH - 1, 0.0, pltpu.roll(middle, WIDTH - 1, 1))
        behind = jnp.where(lane == 0, 0.0, pltpu.roll(middle, 1, 1))
        empty = jnp.zeros((KBLOCK - 3 * SLAB, WIDTH), jnp.float32)
        for col, shifted in enumerate((ahead, middle, behind)):
            for f in range(8):
                slab = jnp.concatenate(
                    [shifted[SLAB * f : SLAB * f + 3 * SLAB], empty], axis=0
                )
                stack[col, g, :, WIDTH * f : WIDTH * (f + 1)] = slab.astype(jnp.bfloat16)
        return carry

    lax.fori_loop(0, HALF, stack_step, 0)

    def grad_step(col, carry):
        sums = [
            lax.dot_general(
                stack[col, g],
                hidden[...],
                (((1,), (1,)), ((), ())),
                preferred_element_type=jnp.float32,
            )
            for g in range(HALF)
        ]
        for a in range(3):
            for b in range(3):
                begin = SLAB * (2 - a) + GROUP * (2 - b)
                piece = jnp.concatenate([s[begin : begin + GROUP] for s in sums], axis=0)
                grad_out[9 * a + 3 * b + col] = piece.astype(jnp.bfloat16)
        return carry

    lax.fori_loop(0, 3, grad_step, 0)

    def part_step(p, carry):
        pixels = pl.ds(pl.multiple_of(p * 256, 256), 256)
        total = jnp.zeros((CHANNELS, 256), jnp.float32)
        for col in range(3):
            for g in range(HALF):
                total = total + lax.dot_general(
                    w[g, KBLOCK * col : KBLOCK * (col + 1), :],
                    stack[col, g, :, pixels],
                    (((0,), (0,)), ((), ())),
                    preferred_element_type=jnp.float32,
                )
        part_out[2 * p] = total[:, :WIDTH]
        part_out[2 * p + 1] = total[:, WIDTH:]
        return carry

    lax.fori_loop(0, 4, part_step, 0)


def compute(adj, x, gain, w):
    return pl.pallas_call(
        compute_kernel,
        out_shape=(
            jax.ShapeDtypeStruct((TAPS, HALF * GROUP, CHANNELS), jnp.bfloat16),
            jax.ShapeDtypeStruct((8, CHANNELS, WIDTH), jnp.float32),
        ),
        scratch_shapes=[
            pltpu.VMEM((3, HALF, KBLOCK, 8 * WIDTH), jnp.bfloat16),
            pltpu.VMEM((CHANNELS, 8 * WIDTH), jnp.bfloat16),
        ],
        compiler_params=pltpu.CompilerParams(vmem_limit_bytes=VMEM_LIMIT),
    )(adj, x, gain, w)


def finish_kernel(
    grad, part, x, gain, x_grad, w_grad, grad_in, part_in, staged, red, red_in, final, sems, local
):
    r = lax.axis_index("rows")
    c = lax.axis_index("chan")
    h = c // 2
    k = lax.rem(c, 2)
    grad_s, grad_r, part_s, part_r, out_s, out_r, red_s, red_r, fin_s, fin_r = [
        sems.at[i] for i in range(10)
    ]
    greet(r, c)

    def grad_send(d, carry):
        target = lax.rem(r + d, ROWS)

        @pl.when(target < TAPS)
        def _():
            send(grad.at[target], grad_in.at[r], grad_s, grad_r, {"rows": target})

        return carry

    part_away = part.at[pl.ds(4 * (1 - k), 4)]
    send(part_away, part_in, part_s, part_r, {"chan": c + 1 - 2 * k})
    lax.fori_loop(1, ROWS, grad_send, 0)

    drain(part_in, part_r)
    gains = gain[...]
    mine = [
        x[g, pl.ds(pl.multiple_of(k * 96, 32), 96), :].astype(jnp.float32) for g in range(CHAN)
    ]
    results = []
    for f in range(4):
        values = jnp.concatenate([m[GROUP * f : GROUP * f + GROUP] for m in mine], axis=0)
        scale, normed = norm_of(values, gains)
        s = sigmoid(normed)
        adjoint = part[4 * k + f] + part_in[f]
        normed_adjoint = adjoint * s * (1.0 + normed * (1.0 - s)) * gains
        projection = jnp.sum(normed_adjoint * values, axis=0, keepdims=True)
        results.append(
            scale * normed_adjoint - values * (scale * scale * scale * projection / CHANNELS)
        )
    for g in range(CHAN):
        rows = jnp.concatenate([y[GROUP * g : GROUP * g + GROUP] for y in results], axis=0)
        staged[g] = rows.astype(jnp.bfloat16)

    here = pl.ds(pl.multiple_of(c * 96, 32), 96)

    def out_step(d, carry):
        target = lax.rem(c + d, CHAN)
        send(staged.at[target], x_grad.at[here], out_s, out_r, {"chan": target})
        return carry

    lax.fori_loop(1, CHAN, out_step, 0)
    own_out = pltpu.make_async_copy(staged.at[c], x_grad.at[here], local.at[0])
    own_out.start()

    @pl.when(r < TAPS)
    def _():
        own_grad = pltpu.make_async_copy(grad.at[r], grad_in.at[r], local.at[1])
        own_grad.start()
        own_grad.wait()
        drain(grad_in.at[pl.ds(0, ROWS - 1)], grad_r)

        def add_step(i, total):
            return total + grad_in[i].astype(jnp.float32)

        total = lax.fori_loop(
            0, ROWS, add_step, jnp.zeros((HALF * GROUP, CHANNELS), jnp.float32)
        )
        for g in range(HALF):
            red[g] = total[GROUP * g : GROUP * (g + 1)]

        def red_step(d, carry):
            target = lax.rem(c + 2 * d, CHAN)
            send(red.at[target // 2], red_in.at[h], red_s, red_r, {"chan": target})
            return carry

        lax.fori_loop(1, HALF, red_step, 0)
        own_red = pltpu.make_async_copy(red.at[h], red_in.at[h], local.at[2])
        own_red.start()
        own_red.wait()
        drain(red_in.at[pl.ds(0, HALF - 1)], red_r)
        whole = red_in[0] + red_in[1] + red_in[2] + red_in[3]
        final[...] = whole * float(ROWS * ROWS * WIDTH) ** (-0.5)

        def final_step(d, carry):
            target = lax.rem(r + d, ROWS)
            send(final, w_grad.at[r], fin_s, fin_r, {"rows": target})
            return carry

        lax.fori_loop(1, ROWS, final_step, 0)
        own_final = pltpu.make_async_copy(final, w_grad.at[r], local.at[3])
        own_final.start()
        own_final.wait()
        drain(grad.at[pl.ds(0, TAPS - 1)], grad_s)
        drain(red.at[pl.ds(0, HALF - 1)], red_s)
        drain(w_grad.at[pl.ds(0, TAPS - 1)], fin_r)

        def sent_step(d, carry):
            drain(final, fin_s)
            return carry

        lax.fori_loop(1, ROWS, sent_step, 0)

    @pl.when(r >= TAPS)
    def _():
        drain(grad.at[pl.ds(0, TAPS)], grad_s)
        drain(w_grad.at[pl.ds(0, TAPS)], fin_r)

    drain(part_in, part_s)
    own_out.wait()
    drain(staged.at[pl.ds(0, CHAN - 1)], out_s)
    drain(x_grad.at[pl.ds(0, (CHAN - 1) * 96)], out_r)


def finish(grad, part, x, gain):
    anywhere = pl.BlockSpec(memory_space=pl.ANY)
    vmem = pl.BlockSpec(memory_space=pltpu.VMEM)
    return pl.pallas_call(
        finish_kernel,
        out_shape=(
            jax.ShapeDtypeStruct((ROWS * GROUP, WIDTH), jnp.bfloat16),
            jax.ShapeDtypeStruct((TAPS, GROUP, CHANNELS), jnp.float32),
        ),
        in_specs=[vmem] * 4,
        out_specs=(anywhere, anywhere),
        scratch_shapes=[
            pltpu.VMEM((ROWS, HALF * GROUP, CHANNELS), jnp.bfloat16),
            pltpu.VMEM((4, CHANNELS, WIDTH), jnp.float32),
            pltpu.VMEM((CHAN, 4 * GROUP, WIDTH), jnp.bfloat16),
            pltpu.VMEM((HALF, GROUP, CHANNELS), jnp.float32),
            pltpu.VMEM((HALF, GROUP, CHANNELS), jnp.float32),
            pltpu.VMEM((GROUP, CHANNELS), jnp.float32),
            pltpu.SemaphoreType.DMA((10,)),
            pltpu.SemaphoreType.DMA((4,)),
        ],
        compiler_params=pltpu.CompilerParams(
            collective_id=1, has_side_effects=True, vmem_limit_bytes=VMEM_LIMIT
        ),
    )(grad, part, x, gain)


def shards(frame_adjoint, frame_slot, inputs, gain, weight):
    slots = jnp.arange(ROWS, dtype=jnp.int32)
    inverse = jnp.sum(jnp.where(frame_slot[None, :] == slots[:, None], slots[None, :], 0), axis=1)
    by_row = jnp.pad(jnp.transpose(frame_adjoint[0], (1, 0, 2)), ((1, 1), (0, 0), (0, 0)))
    windows = jnp.concatenate(
        [by_row[:ROWS], by_row[1 : ROWS + 1], by_row[2:], jnp.zeros((ROWS, 8, WIDTH), jnp.bfloat16)],
        axis=1,
    )
    taps = weight.reshape(3, 3, 3, GROUP, CHANNELS)[::-1, ::-1]
    taps = jnp.transpose(taps, (2, 0, 1, 3, 4)).reshape(3, 3 * SLAB, CHANNELS)
    taps = jnp.pad(taps, ((0, 0), (0, KBLOCK - 3 * SLAB), (0, 0))).reshape(3 * KBLOCK, CHANNELS)
    values = inputs.reshape(ROWS * GROUP, WIDTH)
    gains = jnp.broadcast_to(gain[:, None], (GROUP, WIDTH))
    adj, x, gain_all, w = exchange(inverse, windows, values, gains, taps)
    gain_all = gain_all.reshape(CHANNELS, WIDTH)
    grad, part = compute(adj, x, gain_all, w)
    input_adjoint, weight_adjoint = finish(grad, part, x, gain_all)
    return input_adjoint.reshape(ROWS, GROUP, 1, WIDTH), weight_adjoint


def solution(mesh):
    in_specs = (
        P("rows", "chan", None, None),
        P(),
        P(None, "chan", "rows", None),
        P("chan"),
        P(None, "chan", None),
    )
    out_specs = (P(None, "chan", "rows", None), P(None, "chan", None))
    return jax.shard_map(shards, mesh=mesh, in_specs=in_specs, out_specs=out_specs, check_vma=False)
```

```python
import jax
import jax.numpy as jnp
from jax import lax
from jax.experimental import pallas as pl
from jax.experimental.pallas import tpu as pltpu
from jax.sharding import PartitionSpec as P

CHANNELS = 192
GROUP = 24
WIDTH = 128
ROWS = 32
CHAN = 8
HALF = 4
RING = 4
TAPS = 27
WINDOW = 80
SLAB = 72
KBLOCK = 224
PACK = 1024
LOW = 3 * KBLOCK
PIECE = PACK // ROWS
SLICE = PACK // 8
EPSILON = 1e-06
MESH = pl.DeviceIdType.MESH
VMEM_LIMIT = 56 * 1024 * 1024


def greet(rows_me, chan_me):
    barrier = pltpu.get_barrier_semaphore()

    def rows_step(d, carry):
        pl.semaphore_signal(
            barrier, inc=1, device_id={"rows": lax.rem(rows_me + d, ROWS)}, device_id_type=MESH
        )
        return carry

    def chan_step(d, carry):
        pl.semaphore_signal(
            barrier, inc=1, device_id={"chan": lax.rem(chan_me + d, CHAN)}, device_id_type=MESH
        )
        return carry

    lax.fori_loop(1, ROWS, rows_step, 0)
    lax.fori_loop(1, CHAN, chan_step, 0)
    pl.semaphore_wait(barrier, ROWS - 1 + CHAN - 1)


def send(src, dst, send_sem, recv_sem, device):
    pltpu.make_async_remote_copy(
        src_ref=src,
        dst_ref=dst,
        send_sem=send_sem,
        recv_sem=recv_sem,
        device_id=device,
        device_id_type=MESH,
    ).start()


def drain(ref, sem):
    pltpu.make_async_copy(ref, ref, sem).wait()


def loop(low, high, step):
    def body(i, carry):
        step(i)
        return carry

    lax.fori_loop(low, high, body, 0)


def norm_of(values, gain):
    squares = jnp.sum(values * values, axis=0, keepdims=True)
    scale = lax.rsqrt(squares / CHANNELS + EPSILON)
    return scale, values * scale * gain


def sigmoid(v):
    return 1.0 / (1.0 + jnp.exp(-v))


def pair_lanes(low):
    return jnp.concatenate([low[: KBLOCK // 2], low[KBLOCK // 2 :]], axis=1)


def kernel(
    slot,
    gain,
    frames,
    x,
    w,
    x_grad,
    w_grad,
    wide,
    inverse,
    win,
    recv,
    ordered,
    adj,
    x_all,
    gain_all,
    w_all,
    stack,
    hidden,
    part,
    part_in,
    grad,
    grad_in,
    staged,
    red,
    red_in,
    final,
    win_s,
    win_r,
    x_s,
    x_r,
    gain_s,
    gain_r,
    core_s,
    core_r,
    w_s,
    w_r,
    w2_s,
    w2_r,
    a_s,
    a_r,
    grad_s,
    grad_r,
    part_s,
    part_r,
    out_s,
    out_r,
    red_s,
    red_r,
    fin_s,
    fin_r,
    local,
):
    r = lax.axis_index("rows")
    c = lax.axis_index("chan")
    h = c // 2
    k = lax.rem(c, 2)
    chip_x = r // 8
    chip_y = lax.rem(r, 8) // 2
    other = {"chan": c + 1 - 2 * k}

    wide[...] = frames[...].astype(jnp.float32)

    def win_build(i):
        after = wide[pl.ds(jnp.minimum(i + 1, ROWS - 1), GROUP, stride=ROWS), :]
        here = wide[pl.ds(i, GROUP, stride=ROWS), :]
        before = wide[pl.ds(jnp.maximum(i - 1, 0), GROUP, stride=ROWS), :]
        after = jnp.where(i == ROWS - 1, 0.0, after)
        before = jnp.where(i == 0, 0.0, before)
        empty = jnp.zeros((WINDOW - SLAB, WIDTH), jnp.float32)
        win[i] = jnp.concatenate([after, here, before, empty], axis=0).astype(jnp.bfloat16)

    loop(0, ROWS, win_build)
    recv[r] = win[r]
    x_all[k, 0] = x[pl.ds(pl.multiple_of(h * 192, 64), 192), :]
    gain_all[k, 0] = jnp.concatenate(
        [jnp.full((1, WIDTH), gain[j], jnp.float32) for j in range(GROUP)], axis=0
    )
    for col in range(3):
        rows = [w[9 * a + 3 * b + col].astype(jnp.float32) for a in range(3) for b in range(3)]
        rows = jnp.concatenate(
            rows + [jnp.zeros((KBLOCK - 3 * SLAB, CHANNELS), jnp.float32)], axis=0
        )
        w_all[0, KBLOCK * col : KBLOCK * (col + 1), :] = rows[:, :WIDTH].astype(jnp.bfloat16)
        begin = LOW + KBLOCK // 2 * col
        w_all[0, begin : begin + KBLOCK // 2, :] = pair_lanes(rows[:, WIDTH:]).astype(jnp.bfloat16)
    w_all[0, PACK - 16 :, :] = jnp.zeros((16, WIDTH), jnp.bfloat16)
    ordered[pl.ds(32 * SLAB, 2 * SLAB), :] = jnp.zeros((2 * SLAB, WIDTH), jnp.bfloat16)

    greet(r, c)

    def win_send(d):
        target = lax.rem(r + d, ROWS)
        send(win.at[target], recv.at[r], win_s, win_r, {"rows": target})

    along_x = pl.ds(pl.multiple_of(SLICE * chip_x, SLICE), SLICE)
    along_y = pl.ds(pl.multiple_of(SLICE * (RING + chip_y), SLICE), SLICE)

    def x_send(d):
        target = lax.rem(c + 2 * d, CHAN)
        begin = pl.multiple_of((target // 2) * 192, 64)
        send(x.at[pl.ds(begin, 192)], x_all.at[k, HALF - d], x_s, x_r, {"chan": target})
        send(gain_all.at[k, 0], gain_all.at[k, HALF - d], gain_s, gain_r, {"chan": target})

    def w_send(d):
        target = lax.rem(c + 2 * d, CHAN)
        for rows in (along_x, along_y):
            send(w_all.at[0, rows], w_all.at[HALF - d, rows], w_s, w_r, {"chan": target})

    loop(1, HALF, x_send)
    loop(1, ROWS, win_send)
    loop(1, HALF, w_send)

    def invert(t):
        place = jnp.int32(0)
        for j in range(ROWS):
            place = jnp.where(slot[j] == t, j, place)
        inverse[t] = place

    loop(0, ROWS, invert)

    drain(x_all.at[k, pl.ds(1, HALF - 1)], x_r)
    drain(gain_all.at[k, pl.ds(1, HALF - 1)], gain_r)
    send(x_all.at[k], x_all.at[k], core_s.at[0], core_r.at[0], other)
    send(gain_all.at[k], gain_all.at[k], core_s.at[1], core_r.at[1], other)

    drain(recv.at[pl.ds(0, ROWS - 1)], win_r)

    def order_step(p):
        low = recv[inverse[2 * p]].astype(jnp.float32)[:SLAB]
        high = recv[inverse[2 * p + 1]].astype(jnp.float32)[:SLAB]
        both = jnp.concatenate([low, high], axis=0).astype(jnp.bfloat16)
        ordered[pl.ds(pl.multiple_of(p * 2 * SLAB, 2 * SLAB), 2 * SLAB), :] = both

    loop(0, ROWS // 2, order_step)

    def a_send(d):
        target = lax.rem(c + 2 * d, CHAN)
        start = pl.multiple_of((target // 2) * (8 * SLAB), 64)
        send(
            ordered.at[pl.ds(start, 10 * SLAB)],
            adj.at[HALF - d],
            a_s,
            a_r.at[HALF - d],
            {"chan": target},
        )

    for d in (1, 3, 2):
        a_send(d)
    adj[0] = ordered[pl.ds(pl.multiple_of(h * (8 * SLAB), 64), 10 * SLAB), :]

    drain(w_all.at[pl.ds(1, HALF - 1), pl.ds(0, 2 * SLICE)], w_r)

    def w_spread(d):
        to_x = lax.rem(chip_x + d, RING) * 8 + lax.rem(r, 8)
        to_y = chip_x * 8 + lax.rem(lax.rem(r, 8) + 2 * d, 8)
        for rows, target in ((along_x, to_x), (along_y, to_y)):
            block = w_all.at[pl.ds(1, HALF - 1), rows]
            send(block, block, w2_s, w2_r, {"rows": target})

    loop(1, RING, w_spread)

    drain(x_all.at[1 - k], core_r.at[0])
    drain(gain_all.at[1 - k], core_r.at[1])

    def block_of(channel_group):
        return channel_group % 2, lax.rem(channel_group // 2 - h + HALF, HALF)

    gains = jnp.concatenate([gain_all[block_of(g)] for g in range(CHAN)], axis=0)
    for f in range(8):
        values = jnp.concatenate(
            [
                x_all[block_of(g)].astype(jnp.float32)[GROUP * f : GROUP * f + GROUP]
                for g in range(CHAN)
            ],
            axis=0,
        )
        _, normed = norm_of(values, gains)
        hidden[:, WIDTH * f : WIDTH * (f + 1)] = (normed * sigmoid(normed)).astype(jnp.bfloat16)

    part[...] = jnp.zeros((8, CHANNELS, WIDTH), jnp.float32)
    lane = lax.broadcasted_iota(jnp.int32, (10 * SLAB, WIDTH), 1)

    def block_step(d):
        middle = adj[d].astype(jnp.float32)
        ahead = jnp.where(lane == WIDTH - 1, 0.0, pltpu.roll(middle, WIDTH - 1, 1))
        behind = jnp.where(lane == 0, 0.0, pltpu.roll(middle, 1, 1))
        empty = jnp.zeros((KBLOCK - 3 * SLAB, WIDTH), jnp.float32)
        for col, shifted in enumerate((ahead, middle, behind)):
            for f in range(8):
                slab = jnp.concatenate(
                    [shifted[SLAB * (f + 2 - a) : SLAB * (f + 3 - a)] for a in range(3)] + [empty],
                    axis=0,
                )
                stack[col, :, WIDTH * f : WIDTH * (f + 1)] = slab.astype(jnp.bfloat16)

        def grad_step(col):
            sums = lax.dot_general(
                stack[col],
                hidden[...],
                (((1,), (1,)), ((), ())),
                preferred_element_type=jnp.float32,
            )
            top = pl.ds(pl.multiple_of(KBLOCK * col, 32), KBLOCK)
            grad[d, top, :] = sums[:, :WIDTH].astype(jnp.bfloat16)
            bottom = pl.ds(pl.multiple_of(LOW + KBLOCK // 2 * col, 16), KBLOCK // 2)
            grad[d, bottom, :] = pair_lanes(sums[:, WIDTH:]).astype(jnp.bfloat16)

        loop(0, 3, grad_step)
        grad[d, PACK - 16 :, :] = jnp.zeros((16, WIDTH), jnp.bfloat16)
        grad_in[d, r] = grad[d, pl.ds(pl.multiple_of(r * PIECE, PIECE), PIECE), :]

        def grad_send(e):
            target = lax.rem(r + e, ROWS)
            rows = pl.ds(pl.multiple_of(target * PIECE, PIECE), PIECE)
            send(grad.at[d, rows], grad_in.at[d, r], grad_s, grad_r, {"rows": target})

        loop(1, ROWS, grad_send)

    def part_step(d):
        top = []
        bottom = []
        for col in range(3):
            top.append(w_all[d, KBLOCK * col : KBLOCK * (col + 1), :])
            begin = LOW + KBLOCK // 2 * col
            low = w_all[d, begin : begin + KBLOCK // 2, :].astype(jnp.float32)
            both = jnp.concatenate([low, pltpu.roll(low, 64, 1)], axis=0)
            bottom.append(both[:, :64].astype(jnp.bfloat16))

        def pixels_step(p):
            pixels = pl.ds(pl.multiple_of(p * 256, 256), 256)

            def product(weights):
                total = None
                for col in range(3):
                    term = lax.dot_general(
                        weights[col],
                        stack[col, :, pixels],
                        (((0,), (0,)), ((), ())),
                        preferred_element_type=jnp.float32,
                    )
                    total = term if total is None else total + term
                return total

            high = product(top)
            rest = product(bottom)
            for i in range(2):
                lanes = slice(WIDTH * i, WIDTH * (i + 1))
                part[2 * p + i, :WIDTH, :] += high[:, lanes]
                part[2 * p + i, WIDTH:, :] += rest[:, lanes]

        loop(0, 4, pixels_step)

    block_step(0)
    part_step(0)
    drain(w_all.at[pl.ds(1, HALF - 1), pl.ds(0, 6 * SLICE)], w2_r)
    for d in (1, 3, 2):
        drain(adj.at[d], a_r.at[d])
        block_step(d)
        part_step(d)

    send(part.at[pl.ds(4 * (1 - k), 4)], part_in, part_s, part_r, other)
    mine = [
        x_all[block_of(g) + (pl.ds(pl.multiple_of(k * 96, 32), 96),)].astype(jnp.float32)
        for g in range(CHAN)
    ]
    drain(part_in, part_r)
    results = []
    for f in range(4):
        values = jnp.concatenate([m[GROUP * f : GROUP * f + GROUP] for m in mine], axis=0)
        scale, normed = norm_of(values, gains)
        s = sigmoid(normed)
        adjoint = part[4 * k + f] + part_in[f]
        normed_adjoint = adjoint * s * (1.0 + normed * (1.0 - s)) * gains
        projection = jnp.sum(normed_adjoint * values, axis=0, keepdims=True)
        results.append(
            scale * normed_adjoint - values * (scale * scale * scale * projection / CHANNELS)
        )
    for g in range(CHAN):
        rows = jnp.concatenate([y[GROUP * g : GROUP * g + GROUP] for y in results], axis=0)
        staged[g] = rows.astype(jnp.bfloat16)

    mine_out = pl.ds(pl.multiple_of(c * 96, 32), 96)

    def out_send(d):
        target = lax.rem(c + d, CHAN)
        send(staged.at[target], x_grad.at[mine_out], out_s, out_r, {"chan": target})

    loop(1, CHAN, out_send)
    own_out = pltpu.make_async_copy(staged.at[c], x_grad.at[mine_out], local.at[0])
    own_out.start()

    drain(grad_in.at[:, pl.ds(0, ROWS - 1)], grad_r)
    for d in range(HALF):

        def add_step(i, total):
            return total + grad_in[d, i].astype(jnp.float32)

        red[d] = lax.fori_loop(0, ROWS, add_step, jnp.zeros((PIECE, WIDTH), jnp.float32))
    red_in[0] = red[0]

    def red_send(d):
        send(red.at[d], red_in.at[HALF - d], red_s, red_r, {"chan": lax.rem(c + 2 * d, CHAN)})

    loop(1, HALF, red_send)
    drain(red_in.at[pl.ds(1, HALF - 1)], red_r)
    whole = red_in[0] + red_in[1] + red_in[2] + red_in[3]
    final[...] = whole * float(ROWS * ROWS * WIDTH) ** (-0.5)

    def final_send(d):
        send(final, w_grad.at[r], fin_s, fin_r, {"rows": lax.rem(r + d, ROWS)})

    loop(1, ROWS, final_send)
    own_final = pltpu.make_async_copy(final, w_grad.at[r], local.at[1])
    own_final.start()

    drain(win.at[pl.ds(0, ROWS - 1)], win_s)
    drain(x_all.at[k, pl.ds(1, HALF - 1)], x_s)
    drain(gain_all.at[k, pl.ds(1, HALF - 1)], gain_s)
    drain(x_all.at[k], core_s.at[0])
    drain(gain_all.at[k], core_s.at[1])
    drain(w_all.at[pl.ds(1, HALF - 1), pl.ds(0, 2 * SLICE)], w_s)
    drain(w_all.at[pl.ds(1, HALF - 1), pl.ds(0, 6 * SLICE)], w2_s)
    drain(adj.at[pl.ds(1, HALF - 1)], a_s)
    drain(grad_in.at[:, pl.ds(0, ROWS - 1)], grad_s)
    drain(part_in, part_s)
    drain(staged.at[pl.ds(0, CHAN - 1)], out_s)
    drain(red.at[pl.ds(1, HALF - 1)], red_s)
    drain(w_grad.at[pl.ds(0, ROWS - 1)], fin_s)
    own_out.wait()
    own_final.wait()
    drain(x_grad.at[pl.ds(0, (CHAN - 1) * 96)], out_r)
    drain(w_grad.at[pl.ds(0, ROWS - 1)], fin_r)


def backward(slot, gain, frames, x, w):
    anywhere = pl.BlockSpec(memory_space=pl.ANY)
    scalars = pl.BlockSpec(memory_space=pltpu.SMEM)
    vmem = pl.BlockSpec(memory_space=pltpu.VMEM)
    bf16, f32 = jnp.bfloat16, jnp.float32
    one = pltpu.SemaphoreType.DMA
    many = lambda n: pltpu.SemaphoreType.DMA((n,))
    return pl.pallas_call(
        kernel,
        out_shape=(
            jax.ShapeDtypeStruct((ROWS * GROUP, WIDTH), bf16),
            jax.ShapeDtypeStruct((ROWS, PIECE, WIDTH), f32),
        ),
        in_specs=[scalars, scalars, vmem, vmem, vmem],
        out_specs=(anywhere, anywhere),
        scratch_shapes=[
            pltpu.VMEM((GROUP * ROWS, WIDTH), f32),
            pltpu.SMEM((ROWS,), jnp.int32),
            pltpu.VMEM((ROWS, WINDOW, WIDTH), bf16),
            pltpu.VMEM((ROWS, WINDOW, WIDTH), bf16),
            pltpu.VMEM((34 * SLAB, WIDTH), bf16),
            pltpu.VMEM((HALF, 10 * SLAB, WIDTH), bf16),
            pltpu.VMEM((2, HALF, 8 * GROUP, WIDTH), bf16),
            pltpu.VMEM((2, HALF, GROUP, WIDTH), f32),
            pltpu.VMEM((HALF, PACK, WIDTH), bf16),
            pltpu.VMEM((3, KBLOCK, 8 * WIDTH), bf16),
            pltpu.VMEM((CHANNELS, 8 * WIDTH), bf16),
            pltpu.VMEM((8, CHANNELS, WIDTH), f32),
            pltpu.VMEM((4, CHANNELS, WIDTH), f32),
            pltpu.VMEM((HALF, PACK, WIDTH), bf16),
            pltpu.VMEM((HALF, ROWS, PIECE, WIDTH), bf16),
            pltpu.VMEM((CHAN, 4 * GROUP, WIDTH), bf16),
            pltpu.VMEM((HALF, PIECE, WIDTH), f32),
            pltpu.VMEM((HALF, PIECE, WIDTH), f32),
            pltpu.VMEM((PIECE, WIDTH), f32),
            one, one, one, one, one, one,
            many(2), many(2),
            one, one, one, one,
            one, many(HALF),
            one, one, one, one, one, one, one, one, one, one,
            many(2),
        ],
        compiler_params=pltpu.CompilerParams(
            collective_id=0, has_side_effects=True, vmem_limit_bytes=VMEM_LIMIT
        ),
    )(slot, gain, frames, x, w)


def unpack_kernel(x_in, w_in, x_out, w_out):
    x_out[...] = x_in[...]
    for col in range(3):
        low = w_in[LOW + KBLOCK // 2 * col : LOW + KBLOCK // 2 * (col + 1), :]
        low = jnp.concatenate([low, pltpu.roll(low, 64, 1)], axis=0)
        for a in range(3):
            for b in range(3):
                begin = SLAB * a + GROUP * b
                top = w_in[KBLOCK * col + begin : KBLOCK * col + begin + GROUP, :]
                w_out[9 * a + 3 * b + col, :, :WIDTH] = top
                w_out[9 * a + 3 * b + col, :, WIDTH:] = low[begin : begin + GROUP, :64]


def unpack(x, w):
    return pl.pallas_call(
        unpack_kernel,
        out_shape=(
            jax.ShapeDtypeStruct((ROWS * GROUP, WIDTH), jnp.bfloat16),
            jax.ShapeDtypeStruct((TAPS, GROUP, CHANNELS), jnp.float32),
        ),
        compiler_params=pltpu.CompilerParams(vmem_limit_bytes=16 * 1024 * 1024),
    )(x, w)


def shards(frame_adjoint, frame_slot, inputs, gain, weight):
    frames = frame_adjoint.reshape(GROUP * ROWS, WIDTH)
    values = inputs.reshape(ROWS * GROUP, WIDTH)
    x_grad, w_grad = backward(frame_slot, gain, frames, values, weight)
    input_adjoint, weight_adjoint = unpack(x_grad, w_grad.reshape(PACK, WIDTH))
    return input_adjoint.reshape(ROWS, GROUP, 1, WIDTH), weight_adjoint


def solution(mesh):
    in_specs = (
        P("rows", "chan", None, None),
        P(),
        P(None, "chan", "rows", None),
        P("chan"),
        P(None, "chan", None),
    )
    out_specs = (P(None, "chan", "rows", None), P(None, "chan", None))
    return jax.shard_map(shards, mesh=mesh, in_specs=in_specs, out_specs=out_specs, check_vma=False)
```

```python
import jax
import jax.numpy as jnp
from jax import lax
from jax.experimental import pallas as pl
from jax.experimental.pallas import tpu as pltpu
from jax.sharding import PartitionSpec as P

CHANNELS = 192
GROUP = 24
WIDTH = 128
ROWS = 32
CHAN = 8
HALF = 4
RING = 4
PLANE = 16
TAPS = 27
PADDED = 32
FRAMES = 10
BLOCK = FRAMES * GROUP
SLAB = 72
KBLOCK = 224
PACK = 1024
LOW = 3 * KBLOCK
PIECE = PACK // ROWS
SLICE = PACK // RING
SHARE = PACK // PLANE
EPSILON = 1e-06
MESH = pl.DeviceIdType.MESH
VMEM_LIMIT = 56 * 1024 * 1024


def owner_of(row):
    return lax.rem(row, PLANE) * 2 + row // PLANE


def row_of(rows_index):
    return lax.rem(rows_index, 2) * PLANE + rows_index // 2


def greet_all(r, c):
    barrier = pltpu.get_barrier_semaphore()

    def tell(rows_index, chan_index):
        pl.semaphore_signal(
            barrier, inc=1, device_id=(rows_index, chan_index), device_id_type=MESH
        )

    def chan_step(d):
        chan_index = lax.rem(c + d, CHAN)
        tell(r, chan_index)
        tell(owner_of(r), chan_index)
        tell(row_of(r), chan_index)

    loop(1, ROWS, lambda d: tell(lax.rem(r + d, ROWS), c))
    loop(1, CHAN, chan_step)
    loop(1, HALF, lambda d: tell(r + 1 - 2 * lax.rem(r, 2), lax.rem(c + 2 * d, CHAN)))
    return barrier, ROWS - 1 + 3 * (CHAN - 1) + HALF - 1


def send(src, dst, send_sem, recv_sem, device):
    pltpu.make_async_remote_copy(
        src_ref=src,
        dst_ref=dst,
        send_sem=send_sem,
        recv_sem=recv_sem,
        device_id=device,
        device_id_type=MESH,
    ).start()


def drain(ref, sem):
    pltpu.make_async_copy(ref, ref, sem).wait()


def loop(low, high, step):
    def body(i, carry):
        step(i)
        return carry

    lax.fori_loop(low, high, body, 0)


def norm_of(values, gain):
    squares = jnp.sum(values * values, axis=0, keepdims=True)
    scale = lax.rsqrt(squares / CHANNELS + EPSILON)
    return scale, values * scale * gain


def sigmoid(v):
    return 1.0 / (1.0 + jnp.exp(-v))


def pair_lanes(low):
    return jnp.concatenate([low[: KBLOCK // 2], low[KBLOCK // 2 :]], axis=1)


def kernel(
    slot,
    gain,
    frames,
    x,
    w,
    x_grad,
    w_grad,
    wide,
    inverse,
    win,
    recv,
    ordered,
    adj,
    beside,
    x_all,
    gain_all,
    w_all,
    w_turned,
    stack,
    hidden,
    part,
    part_in,
    grad,
    grad_in,
    staged,
    red,
    red_in,
    final,
    win_s,
    win_r,
    x_s,
    x_r,
    gain_s,
    gain_r,
    core_s,
    core_r,
    w_s,
    w_r,
    a_s,
    a_r,
    after_s,
    before_s,
    beside_r,
    grad_s,
    grad_r,
    part_s,
    part_r,
    out_s,
    out_r,
    red_s,
    red_r,
    fin_s,
    fin_r,
    local,
):
    r = lax.axis_index("rows")
    c = lax.axis_index("chan")
    h = c // 2
    k = lax.rem(c, 2)
    z_low = lax.rem(r, 2)
    place = r // 2
    chip_x = r // 8
    row = row_of(r)
    owner = owner_of(r)
    at_home = row == r
    other = {"chan": c + 1 - 2 * k}

    barrier, greetings = greet_all(r, c)

    wide[...] = frames[...].astype(jnp.float32)
    empty = jnp.zeros((PADDED - GROUP, WIDTH), jnp.float32)

    def win_build(i):
        rows = wide[pl.ds(i, GROUP, stride=ROWS), :]
        win[owner_of(i)] = jnp.concatenate([rows, empty], axis=0).astype(jnp.bfloat16)

    loop(0, ROWS, win_build)
    recv[r] = win[r]
    gain_all[k, 0] = jnp.concatenate(
        [jnp.full((1, WIDTH), gain[j], jnp.float32) for j in range(GROUP)], axis=0
    )
    ordered[pl.ds(32 * GROUP, 2 * GROUP), :] = jnp.zeros((2 * GROUP, WIDTH), jnp.bfloat16)

    for col in range(3):
        rows = [w[9 * a + 3 * b + col].astype(jnp.float32) for a in range(3) for b in range(3)]
        rows = jnp.concatenate(
            rows + [jnp.zeros((KBLOCK - 3 * SLAB, CHANNELS), jnp.float32)], axis=0
        )
        w_all[0, KBLOCK * col : KBLOCK * (col + 1), :] = rows[:, :WIDTH].astype(jnp.bfloat16)
        begin = LOW + KBLOCK // 2 * col
        w_all[0, begin : begin + KBLOCK // 2, :] = pair_lanes(rows[:, WIDTH:]).astype(jnp.bfloat16)
    w_all[0, PACK - 16 :, :] = jnp.zeros((16, WIDTH), jnp.bfloat16)

    pl.semaphore_wait(barrier, greetings)

    mine_w = pl.ds(pl.multiple_of(SHARE * place, SHARE), SHARE)
    along_x = pl.ds(pl.multiple_of(SLICE * chip_x, SLICE), SLICE)

    def w_send(d):
        target = lax.rem(c + 2 * d, CHAN)
        send(w_all.at[0, mine_w], w_all.at[HALF - d, mine_w], w_s.at[0], w_r.at[0], {"chan": target})

    def w_spread_y(d):
        block = w_all.at[pl.ds(1, HALF - 1), mine_w]
        target = chip_x * 8 + lax.rem(lax.rem(r, 8) + 2 * d, 8)
        send(block, block, w_s.at[1], w_r.at[1], {"rows": target})

    def w_spread_x(d):
        block = w_all.at[pl.ds(1, HALF - 1), along_x]
        target = lax.rem(chip_x + d, RING) * 8 + lax.rem(r, 8)
        send(block, block, w_s.at[2], w_r.at[2], {"rows": target})

    def win_send(d):
        target = lax.rem(r + d, ROWS)
        send(win.at[target], recv.at[r], win_s, win_r, {"rows": target})

    loop(1, HALF, w_send)
    loop(1, ROWS, win_send)

    def x_send(d):
        target = lax.rem(c + 2 * d, CHAN)
        begin = pl.multiple_of((target // 2) * 192, 64)
        send(
            x.at[pl.ds(begin, 192)],
            x_all.at[k, lax.rem(HALF - d, HALF)],
            x_s,
            x_r,
            (owner, target),
        )

    def gain_send(d):
        target = lax.rem(c + 2 * d, CHAN)
        send(gain_all.at[k, 0], gain_all.at[k, HALF - d], gain_s, gain_r, {"chan": target})

    @pl.when(at_home)
    def _():
        begin = pl.multiple_of(h * 192, 64)
        pltpu.make_async_copy(x.at[pl.ds(begin, 192)], x_all.at[k, 0], x_r).start()

    @pl.when(jnp.logical_not(at_home))
    def _():
        x_send(0)

    loop(1, HALF, x_send)
    loop(1, HALF, gain_send)

    def invert(t):
        found = jnp.int32(0)
        for j in range(ROWS):
            found = jnp.where(slot[j] == t, j, found)
        inverse[t] = found

    loop(0, ROWS, invert)
    drain(w_all.at[pl.ds(1, HALF - 1), pl.ds(0, SHARE)], w_r.at[0])
    loop(1, RING, w_spread_y)
    drain(recv.at[pl.ds(0, ROWS - 1)], win_r)

    def order_step(p):
        low = recv[inverse[2 * p]].astype(jnp.float32)[:GROUP]
        high = recv[inverse[2 * p + 1]].astype(jnp.float32)[:GROUP]
        both = jnp.concatenate([low, high], axis=0).astype(jnp.bfloat16)
        ordered[pl.ds(pl.multiple_of(p * 2 * GROUP, 2 * GROUP), 2 * GROUP), :] = both

    loop(0, ROWS // 2, order_step)

    def a_send(d):
        target = lax.rem(c + 2 * d, CHAN)
        start = pl.multiple_of((target // 2) * (8 * GROUP), 64)
        send(
            ordered.at[pl.ds(start, BLOCK)],
            adj.at[HALF - d],
            a_s,
            a_r.at[HALF - d],
            {"chan": target},
        )

    for d in (1, 3, 2):
        a_send(d)
    adj[0] = ordered[pl.ds(pl.multiple_of(h * (8 * GROUP), 64), BLOCK), :]
    has_after = row < ROWS - 1
    has_before = row > 0

    @pl.when(jnp.logical_not(has_after))
    def _():
        beside[0] = jnp.zeros((HALF, BLOCK, WIDTH), jnp.bfloat16)

    @pl.when(jnp.logical_not(has_before))
    def _():
        beside[1] = jnp.zeros((HALF, BLOCK, WIDTH), jnp.bfloat16)

    def beside_send(d):
        @pl.when(has_after)
        def _():
            target = {"rows": owner_of(row + 1)}
            send(adj.at[d], beside.at[1, d], after_s, beside_r.at[1, d], target)

        @pl.when(has_before)
        def _():
            target = {"rows": owner_of(row - 1)}
            send(adj.at[d], beside.at[0, d], before_s, beside_r.at[0, d], target)

    def beside_wait(d):
        @pl.when(has_after)
        def _():
            drain(beside.at[0, d], beside_r.at[0, d])

        @pl.when(has_before)
        def _():
            drain(beside.at[1, d], beside_r.at[1, d])

    beside_send(0)

    drain(w_all.at[pl.ds(1, HALF - 1), pl.ds(0, 3 * SHARE)], w_r.at[1])
    loop(1, RING, w_spread_x)

    drain(x_all.at[k], x_r)
    drain(gain_all.at[k, pl.ds(1, HALF - 1)], gain_r)
    send(x_all.at[k], x_all.at[k], core_s.at[0], core_r.at[0], other)
    send(gain_all.at[k], gain_all.at[k], core_s.at[1], core_r.at[1], other)

    for d in (1, 3):
        drain(adj.at[d], a_r.at[d])
        beside_send(d)

    drain(x_all.at[1 - k], core_r.at[0])
    drain(gain_all.at[1 - k], core_r.at[1])

    def block_of(channel_group):
        return channel_group % 2, lax.rem(channel_group // 2 - h + HALF, HALF)

    gains = jnp.concatenate([gain_all[block_of(g)] for g in range(CHAN)], axis=0)
    for f in range(8):
        values = jnp.concatenate(
            [
                x_all[block_of(g)].astype(jnp.float32)[GROUP * f : GROUP * f + GROUP]
                for g in range(CHAN)
            ],
            axis=0,
        )
        _, normed = norm_of(values, gains)
        turned = jnp.transpose(normed * sigmoid(normed))
        hidden[WIDTH * f : WIDTH * (f + 1), :] = turned.astype(jnp.bfloat16)

    drain(adj.at[2], a_r.at[2])
    beside_send(2)

    lane = lax.broadcasted_iota(jnp.int32, (BLOCK, WIDTH), 1)

    def stack_step(d):
        three = [beside[0, d], adj[d], beside[1, d]]
        three = [v.astype(jnp.float32) for v in three]
        filler = jnp.zeros((KBLOCK - 3 * SLAB, WIDTH), jnp.float32)
        for col in range(3):
            if col == 0:
                moved = [
                    jnp.where(lane == WIDTH - 1, 0.0, pltpu.roll(v, WIDTH - 1, 1)) for v in three
                ]
            elif col == 1:
                moved = three
            else:
                moved = [jnp.where(lane == 0, 0.0, pltpu.roll(v, 1, 1)) for v in three]
            for f in range(8):
                slab = jnp.concatenate(
                    [
                        moved[b][GROUP * (f + 2 - a) : GROUP * (f + 3 - a)]
                        for a in range(3)
                        for b in range(3)
                    ]
                    + [filler],
                    axis=0,
                )
                stack[d, KBLOCK * col : KBLOCK * (col + 1), WIDTH * f : WIDTH * (f + 1)] = (
                    slab.astype(jnp.bfloat16)
                )

    def grad_step(d):
        sums = jnp.dot(stack[d], hidden[...], preferred_element_type=jnp.float32)
        grad[d, :LOW, :] = sums[:, :WIDTH].astype(jnp.bfloat16)
        for col in range(3):
            begin = LOW + KBLOCK // 2 * col
            low = sums[KBLOCK * col : KBLOCK * (col + 1), WIDTH:]
            grad[d, begin : begin + KBLOCK // 2, :] = pair_lanes(low).astype(jnp.bfloat16)
        grad[d, PACK - 16 :, :] = jnp.zeros((16, WIDTH), jnp.bfloat16)
        grad_in[d, place] = grad[d, pl.ds(pl.multiple_of(place * SHARE, SHARE), SHARE), :]

        def grad_send(e):
            target = lax.rem(place + e, PLANE)
            rows = pl.ds(pl.multiple_of(target * SHARE, SHARE), SHARE)
            send(
                grad.at[d, rows],
                grad_in.at[d, place],
                grad_s,
                grad_r.at[d],
                {"rows": target * 2 + z_low},
            )

        loop(1, PLANE, grad_send)

    def turn_weights(d):
        blocks = []
        for col in range(3):
            top = w_all[d, KBLOCK * col : KBLOCK * (col + 1), :].astype(jnp.float32)
            begin = LOW + KBLOCK // 2 * col
            low = w_all[d, begin : begin + KBLOCK // 2, :].astype(jnp.float32)
            low = jnp.concatenate([low, pltpu.roll(low, 64, 1)], axis=0)
            blocks.append((top, low))
        top = jnp.transpose(jnp.concatenate([b[0] for b in blocks], axis=0))
        low = jnp.transpose(jnp.concatenate([b[1] for b in blocks], axis=0))
        w_turned[d, :WIDTH, :] = top.astype(jnp.bfloat16)
        w_turned[d, WIDTH:, :] = low[:64].astype(jnp.bfloat16)

    def part_step(p):
        pixels = pl.ds(pl.multiple_of(p * 256, 256), 256)
        total = None
        for d in range(HALF):
            term = jnp.dot(w_turned[d], stack[d, :, pixels], preferred_element_type=jnp.float32)
            total = term if total is None else total + term
        part[2 * p] = total[:, :WIDTH]
        part[2 * p + 1] = total[:, WIDTH:]

    for d in (0, 1, 3, 2):
        beside_wait(d)
        stack_step(d)
        grad_step(d)
        if d == 0:
            turn_weights(0)
    drain(w_all.at[pl.ds(1, HALF - 1), pl.ds(0, 3 * SLICE)], w_r.at[2])
    loop(1, HALF, turn_weights)
    loop(2 * (1 - k), 2 * (1 - k) + 2, part_step)
    send(part.at[pl.ds(4 * (1 - k), 4)], part_in, part_s, part_r, other)
    loop(2 * k, 2 * k + 2, part_step)

    def reduce_step(d):
        drain(grad_in.at[d, pl.ds(0, PLANE - 1)], grad_r.at[d])

        def add_step(i, total):
            return total + grad_in[d, i].astype(jnp.float32)

        red[d] = lax.fori_loop(0, PLANE, add_step, jnp.zeros((SHARE, WIDTH), jnp.float32))

    reduce_step(0)
    mine = [
        x_all[block_of(g) + (pl.ds(pl.multiple_of(k * 96, 32), 96),)].astype(jnp.float32)
        for g in range(CHAN)
    ]
    drain(part_in, part_r)
    results = []
    for f in range(4):
        values = jnp.concatenate([m[GROUP * f : GROUP * f + GROUP] for m in mine], axis=0)
        scale, normed = norm_of(values, gains)
        s = sigmoid(normed)
        adjoint = part[4 * k + f] + part_in[f]
        normed_adjoint = adjoint * s * (1.0 + normed * (1.0 - s)) * gains
        projection = jnp.sum(normed_adjoint * values, axis=0, keepdims=True)
        results.append(
            scale * normed_adjoint - values * (scale * scale * scale * projection / CHANNELS)
        )
    for g in range(CHAN):
        rows = jnp.concatenate([y[GROUP * g : GROUP * g + GROUP] for y in results], axis=0)
        staged[g] = rows.astype(jnp.bfloat16)

    mine_out = pl.ds(pl.multiple_of(c * 96, 32), 96)

    def out_send(d):
        target = lax.rem(c + d, CHAN)
        send(staged.at[target], x_grad.at[mine_out], out_s, out_r, (row, target))

    @pl.when(at_home)
    def _():
        pltpu.make_async_copy(staged.at[c], x_grad.at[mine_out], out_r).start()

    @pl.when(jnp.logical_not(at_home))
    def _():
        out_send(0)

    loop(1, CHAN, out_send)

    for d in (1, 3, 2):
        reduce_step(d)
    red_in[z_low * HALF] = red[0, pl.ds(pl.multiple_of(z_low * PIECE, PIECE), PIECE), :]

    def red_send(d, chip_z):
        rows = pl.ds(pl.multiple_of(chip_z * PIECE, PIECE), PIECE)
        send(
            red.at[d, rows],
            red_in.at[z_low * HALF + lax.rem(HALF - d, HALF)],
            red_s,
            red_r,
            (r - z_low + chip_z, lax.rem(c + 2 * d, CHAN)),
        )

    loop(1, HALF, lambda d: red_send(d, z_low))
    loop(0, HALF, lambda d: red_send(d, 1 - z_low))
    drain(red_in.at[pl.ds(0, CHAN - 1)], red_r)
    whole = jnp.zeros((PIECE, WIDTH), jnp.float32)
    for i in range(CHAN):
        whole = whole + red_in[i]
    final[...] = whole * float(ROWS * ROWS * WIDTH) ** (-0.5)

    def final_send(d):
        send(final, w_grad.at[r], fin_s, fin_r, {"rows": lax.rem(r + d, ROWS)})

    loop(1, ROWS, final_send)
    own_final = pltpu.make_async_copy(final, w_grad.at[r], local)
    own_final.start()

    drain(win.at[pl.ds(0, ROWS - 1)], win_s)
    drain(gain_all.at[k, pl.ds(1, HALF - 1)], gain_s)
    drain(x_all.at[k], core_s.at[0])
    drain(gain_all.at[k], core_s.at[1])
    drain(w_all.at[pl.ds(1, HALF - 1), pl.ds(0, SHARE)], w_s.at[0])
    drain(w_all.at[pl.ds(1, HALF - 1), pl.ds(0, 3 * SHARE)], w_s.at[1])
    drain(w_all.at[pl.ds(1, HALF - 1), pl.ds(0, 3 * SLICE)], w_s.at[2])
    drain(adj.at[pl.ds(1, HALF - 1)], a_s)

    @pl.when(has_after)
    def _():
        drain(adj, after_s)

    @pl.when(has_before)
    def _():
        drain(adj, before_s)

    drain(grad_in.at[:, pl.ds(0, PLANE - 1)], grad_s)
    drain(part_in, part_s)

    @pl.when(at_home)
    def _():
        drain(x_all.at[k, pl.ds(1, HALF - 1)], x_s)
        drain(staged.at[pl.ds(0, CHAN - 1)], out_s)

    @pl.when(jnp.logical_not(at_home))
    def _():
        drain(x_all.at[k], x_s)
        drain(staged, out_s)

    drain(red_in.at[pl.ds(0, CHAN - 1)], red_s)
    drain(w_grad.at[pl.ds(0, ROWS - 1)], fin_s)
    own_final.wait()
    drain(x_grad, out_r)
    drain(w_grad.at[pl.ds(0, ROWS - 1)], fin_r)


def backward(slot, gain, frames, x, w):
    anywhere = pl.BlockSpec(memory_space=pl.ANY)
    scalars = pl.BlockSpec(memory_space=pltpu.SMEM)
    vmem = pl.BlockSpec(memory_space=pltpu.VMEM)
    bf16, f32 = jnp.bfloat16, jnp.float32
    one = pltpu.SemaphoreType.DMA
    many = lambda n: pltpu.SemaphoreType.DMA((n,))
    return pl.pallas_call(
        kernel,
        out_shape=(
            jax.ShapeDtypeStruct((ROWS * GROUP, WIDTH), bf16),
            jax.ShapeDtypeStruct((ROWS, PIECE, WIDTH), f32),
        ),
        in_specs=[scalars, scalars, vmem, vmem, vmem],
        out_specs=(anywhere, anywhere),
        scratch_shapes=[
            pltpu.VMEM((GROUP * ROWS, WIDTH), f32),
            pltpu.SMEM((ROWS,), jnp.int32),
            pltpu.VMEM((ROWS, PADDED, WIDTH), bf16),
            pltpu.VMEM((ROWS, PADDED, WIDTH), bf16),
            pltpu.VMEM((34 * GROUP, WIDTH), bf16),
            pltpu.VMEM((HALF, BLOCK, WIDTH), bf16),
            pltpu.VMEM((2, HALF, BLOCK, WIDTH), bf16),
            pltpu.VMEM((2, HALF, 8 * GROUP, WIDTH), bf16),
            pltpu.VMEM((2, HALF, GROUP, WIDTH), f32),
            pltpu.VMEM((HALF, PACK, WIDTH), bf16),
            pltpu.VMEM((HALF, CHANNELS, LOW), bf16),
            pltpu.VMEM((HALF, LOW, 8 * WIDTH), bf16),
            pltpu.VMEM((8 * WIDTH, CHANNELS), bf16),
            pltpu.VMEM((8, CHANNELS, WIDTH), f32),
            pltpu.VMEM((4, CHANNELS, WIDTH), f32),
            pltpu.VMEM((HALF, PACK, WIDTH), bf16),
            pltpu.VMEM((HALF, PLANE, SHARE, WIDTH), bf16),
            pltpu.VMEM((CHAN, 4 * GROUP, WIDTH), bf16),
            pltpu.VMEM((HALF, SHARE, WIDTH), f32),
            pltpu.VMEM((CHAN, PIECE, WIDTH), f32),
            pltpu.VMEM((PIECE, WIDTH), f32),
            one, one, one, one, one, one,
            many(2), many(2),
            many(3), many(3),
            one, many(HALF),
            one, one, pltpu.SemaphoreType.DMA((2, HALF)),
            one, many(HALF),
            one, one, one, one, one, one, one, one,
            one,
        ],
        compiler_params=pltpu.CompilerParams(
            collective_id=0, has_side_effects=True, vmem_limit_bytes=VMEM_LIMIT
        ),
    )(slot, gain, frames, x, w)


def unpack_kernel(x_in, w_in, x_out, w_out, held_x, held_w, sems):
    x_copy = pltpu.make_async_copy(x_in, held_x, sems.at[0])
    w_copy = pltpu.make_async_copy(w_in, held_w, sems.at[1])
    w_copy.start()
    x_copy.start()
    x_copy.wait()
    x_back = pltpu.make_async_copy(held_x, x_out, sems.at[2])
    x_back.start()
    w_copy.wait()
    for col in range(3):
        low = held_w[LOW + KBLOCK // 2 * col : LOW + KBLOCK // 2 * (col + 1), :]
        low = low.astype(jnp.float32)
        low = jnp.concatenate([low, pltpu.roll(low, 64, 1)], axis=0)
        top = held_w[KBLOCK * col : KBLOCK * (col + 1), :].astype(jnp.float32)
        for a in range(3):
            for b in range(3):
                begin = SLAB * a + GROUP * b
                w_out[9 * a + 3 * b + col, :, :WIDTH] = top[begin : begin + GROUP]
                w_out[9 * a + 3 * b + col, :, WIDTH:] = low[begin : begin + GROUP, :64]
    x_back.wait()


def unpack(x, w):
    anywhere = pl.BlockSpec(memory_space=pl.ANY)
    return pl.pallas_call(
        unpack_kernel,
        out_shape=(
            jax.ShapeDtypeStruct((ROWS * GROUP, WIDTH), jnp.bfloat16),
            jax.ShapeDtypeStruct((TAPS, GROUP, CHANNELS), jnp.float32),
        ),
        in_specs=[anywhere] * 2,
        out_specs=(anywhere, pl.BlockSpec(memory_space=pltpu.VMEM)),
        scratch_shapes=[
            pltpu.VMEM(x.shape, x.dtype),
            pltpu.VMEM(w.shape, w.dtype),
            pltpu.SemaphoreType.DMA((3,)),
        ],
        compiler_params=pltpu.CompilerParams(vmem_limit_bytes=VMEM_LIMIT),
    )(x, w)


def shards(frame_adjoint, frame_slot, inputs, gain, weight):
    frames = frame_adjoint.reshape(GROUP * ROWS, WIDTH)
    values = inputs.reshape(ROWS * GROUP, WIDTH)
    x_grad, w_grad = backward(frame_slot, gain, frames, values, weight)
    input_adjoint, weight_adjoint = unpack(x_grad, w_grad.reshape(PACK, WIDTH))
    return input_adjoint.reshape(ROWS, GROUP, 1, WIDTH), weight_adjoint


def solution(mesh):
    in_specs = (
        P("rows", "chan", None, None),
        P(),
        P(None, "chan", "rows", None),
        P("chan"),
        P(None, "chan", None),
    )
    out_specs = (P(None, "chan", "rows", None), P(None, "chan", None))
    return jax.shard_map(shards, mesh=mesh, in_specs=in_specs, out_specs=out_specs, check_vma=False)
```

```python
import jax
import jax.numpy as jnp
from jax import lax
from jax.experimental import pallas as pl
from jax.experimental.pallas import tpu as pltpu
from jax.sharding import PartitionSpec as P

CHANNELS = 192
GROUP = 24
WIDTH = 128
ROWS = 32
CHAN = 8
HALF = 4
RING = 4
PLANE = 16
TAPS = 27
PADDED = 32
FRAMES = 10
BLOCK = FRAMES * GROUP
SLAB = 72
KBLOCK = 224
PACK = 1024
LOW = 3 * KBLOCK
PIECE = PACK // ROWS
SLICE = PACK // RING
SHARE = PACK // PLANE
EPSILON = 1e-06
MESH = pl.DeviceIdType.MESH
VMEM_LIMIT = 56 * 1024 * 1024


def owner_of(row):
    return row + lax.rem(row % 8 // 2, 2) * (1 - 2 * lax.rem(row, 2))


def greet_all(r, c):
    barrier = pltpu.get_barrier_semaphore()

    def tell(rows_index, chan_index):
        pl.semaphore_signal(
            barrier, inc=1, device_id=(rows_index, chan_index), device_id_type=MESH
        )

    def chan_step(d):
        chan_index = lax.rem(c + d, CHAN)
        tell(r, chan_index)
        tell(r + 1 - 2 * lax.rem(r, 2), chan_index)

    loop(1, ROWS, lambda d: tell(lax.rem(r + d, ROWS), c))
    loop(1, CHAN, chan_step)
    return barrier, ROWS - 1 + 2 * (CHAN - 1)


def send(src, dst, send_sem, recv_sem, device):
    pltpu.make_async_remote_copy(
        src_ref=src,
        dst_ref=dst,
        send_sem=send_sem,
        recv_sem=recv_sem,
        device_id=device,
        device_id_type=MESH,
    ).start()


def drain(ref, sem):
    pltpu.make_async_copy(ref, ref, sem).wait()


def loop(low, high, step):
    def body(i, carry):
        step(i)
        return carry

    lax.fori_loop(low, high, body, 0)


def norm_of(values, gain):
    squares = jnp.sum(values * values, axis=0, keepdims=True)
    scale = lax.rsqrt(squares / CHANNELS + EPSILON)
    return scale, values * scale * gain


def sigmoid(v):
    return 1.0 / (1.0 + jnp.exp(-v))


def pair_lanes(low):
    return jnp.concatenate([low[: KBLOCK // 2], low[KBLOCK // 2 :]], axis=1)


def kernel(
    slot,
    gain,
    frames_in,
    x_in,
    w_in,
    x_grad,
    w_grad,
    frames,
    x,
    w,
    wide,
    inverse,
    win,
    recv,
    ordered,
    adj,
    beside,
    x_all,
    gain_all,
    w_all,
    w_turned,
    stack,
    hidden,
    part,
    part_in,
    grad,
    grad_in,
    staged,
    red,
    red_in,
    final,
    win_s,
    win_r,
    x_s,
    x_r,
    gain_s,
    gain_r,
    core_s,
    core_r,
    w_s,
    w_r,
    a_s,
    a_r,
    after_s,
    before_s,
    beside_r,
    grad_s,
    grad_r,
    part_s,
    part_r,
    out_s,
    out_r,
    red_s,
    red_r,
    fin_s,
    fin_r,
    local,
):
    r = lax.axis_index("rows")
    c = lax.axis_index("chan")
    h = c // 2
    k = lax.rem(c, 2)
    z_low = lax.rem(r, 2)
    place = r // 2
    chip_x = r // 8
    row = owner_of(r)
    at_home = row == r
    other = {"chan": c + 1 - 2 * k}

    fetches = [
        pltpu.make_async_copy(src, dst, local.at[i])
        for i, (src, dst) in enumerate(((frames_in, frames), (w_in, w), (x_in, x)))
    ]
    for fetch in fetches:
        fetch.start()
    barrier, greetings = greet_all(r, c)
    fetches[0].wait()

    wide[...] = frames[...].astype(jnp.float32)
    empty = jnp.zeros((PADDED - GROUP, WIDTH), jnp.float32)

    def win_build(i):
        rows = wide[pl.ds(i, GROUP, stride=ROWS), :]
        win[owner_of(i)] = jnp.concatenate([rows, empty], axis=0).astype(jnp.bfloat16)

    loop(0, ROWS, win_build)
    recv[r] = win[r]
    gain_all[k, 0] = jnp.concatenate(
        [jnp.full((1, WIDTH), gain[j], jnp.float32) for j in range(GROUP)], axis=0
    )
    ordered[pl.ds(32 * GROUP, 2 * GROUP), :] = jnp.zeros((2 * GROUP, WIDTH), jnp.bfloat16)

    fetches[1].wait()
    for col in range(3):
        rows = [w[9 * a + 3 * b + col].astype(jnp.float32) for a in range(3) for b in range(3)]
        rows = jnp.concatenate(
            rows + [jnp.zeros((KBLOCK - 3 * SLAB, CHANNELS), jnp.float32)], axis=0
        )
        w_all[0, KBLOCK * col : KBLOCK * (col + 1), :] = rows[:, :WIDTH].astype(jnp.bfloat16)
        begin = LOW + KBLOCK // 2 * col
        w_all[0, begin : begin + KBLOCK // 2, :] = pair_lanes(rows[:, WIDTH:]).astype(jnp.bfloat16)
    w_all[0, PACK - 16 :, :] = jnp.zeros((16, WIDTH), jnp.bfloat16)
    fetches[2].wait()

    pl.semaphore_wait(barrier, greetings)

    mine_w = pl.ds(pl.multiple_of(SHARE * place, SHARE), SHARE)
    along_x = pl.ds(pl.multiple_of(SLICE * chip_x, SLICE), SLICE)

    def w_send(d):
        target = lax.rem(c + 2 * d, CHAN)
        send(w_all.at[0, mine_w], w_all.at[HALF - d, mine_w], w_s.at[0], w_r.at[0], {"chan": target})

    def w_spread_y(d):
        block = w_all.at[pl.ds(1, HALF - 1), mine_w]
        target = chip_x * 8 + lax.rem(lax.rem(r, 8) + 2 * d, 8)
        send(block, block, w_s.at[1], w_r.at[1], {"rows": target})

    def w_spread_x(d):
        block = w_all.at[pl.ds(1, HALF - 1), along_x]
        target = lax.rem(chip_x + d, RING) * 8 + lax.rem(r, 8)
        send(block, block, w_s.at[2], w_r.at[2], {"rows": target})

    def win_send(d):
        target = lax.rem(r + d, ROWS)
        send(win.at[target], recv.at[r], win_s, win_r, {"rows": target})

    loop(1, HALF, w_send)
    loop(1, ROWS, win_send)

    def x_send(d):
        target = lax.rem(c + 2 * d, CHAN)
        begin = pl.multiple_of((target // 2) * 192, 64)
        send(
            x.at[pl.ds(begin, 192)],
            x_all.at[k, lax.rem(HALF - d, HALF)],
            x_s,
            x_r,
            (row, target),
        )

    def gain_send(d):
        target = lax.rem(c + 2 * d, CHAN)
        send(gain_all.at[k, 0], gain_all.at[k, HALF - d], gain_s, gain_r, {"chan": target})

    @pl.when(at_home)
    def _():
        begin = pl.multiple_of(h * 192, 64)
        pltpu.make_async_copy(x.at[pl.ds(begin, 192)], x_all.at[k, 0], x_r).start()

    @pl.when(jnp.logical_not(at_home))
    def _():
        x_send(0)

    loop(1, HALF, x_send)
    loop(1, HALF, gain_send)

    def invert(t):
        found = jnp.int32(0)
        for j in range(ROWS):
            found = jnp.where(slot[j] == t, j, found)
        inverse[t] = found

    loop(0, ROWS, invert)
    drain(w_all.at[pl.ds(1, HALF - 1), pl.ds(0, SHARE)], w_r.at[0])
    loop(1, RING, w_spread_y)
    drain(recv.at[pl.ds(0, ROWS - 1)], win_r)

    def order_step(p):
        low = recv[inverse[2 * p]].astype(jnp.float32)[:GROUP]
        high = recv[inverse[2 * p + 1]].astype(jnp.float32)[:GROUP]
        both = jnp.concatenate([low, high], axis=0).astype(jnp.bfloat16)
        ordered[pl.ds(pl.multiple_of(p * 2 * GROUP, 2 * GROUP), 2 * GROUP), :] = both

    loop(0, ROWS // 2, order_step)

    def a_send(d):
        target = lax.rem(c + 2 * d, CHAN)
        start = pl.multiple_of((target // 2) * (8 * GROUP), 64)
        send(
            ordered.at[pl.ds(start, BLOCK)],
            adj.at[HALF - d],
            a_s,
            a_r.at[HALF - d],
            {"chan": target},
        )

    for d in (1, 3, 2):
        a_send(d)
    adj[0] = ordered[pl.ds(pl.multiple_of(h * (8 * GROUP), 64), BLOCK), :]
    has_after = row < ROWS - 1
    has_before = row > 0

    @pl.when(jnp.logical_not(has_after))
    def _():
        beside[0] = jnp.zeros((HALF, BLOCK, WIDTH), jnp.bfloat16)

    @pl.when(jnp.logical_not(has_before))
    def _():
        beside[1] = jnp.zeros((HALF, BLOCK, WIDTH), jnp.bfloat16)

    def beside_send(d):
        @pl.when(has_after)
        def _():
            target = {"rows": owner_of(row + 1)}
            send(adj.at[d], beside.at[1, d], after_s, beside_r.at[1, d], target)

        @pl.when(has_before)
        def _():
            target = {"rows": owner_of(row - 1)}
            send(adj.at[d], beside.at[0, d], before_s, beside_r.at[0, d], target)

    def beside_wait(d):
        @pl.when(has_after)
        def _():
            drain(beside.at[0, d], beside_r.at[0, d])

        @pl.when(has_before)
        def _():
            drain(beside.at[1, d], beside_r.at[1, d])

    beside_send(0)

    drain(w_all.at[pl.ds(1, HALF - 1), pl.ds(0, 3 * SHARE)], w_r.at[1])
    loop(1, RING, w_spread_x)

    drain(x_all.at[k], x_r)
    drain(gain_all.at[k, pl.ds(1, HALF - 1)], gain_r)
    send(x_all.at[k], x_all.at[k], core_s.at[0], core_r.at[0], other)
    send(gain_all.at[k], gain_all.at[k], core_s.at[1], core_r.at[1], other)

    drain(x_all.at[1 - k], core_r.at[0])
    drain(gain_all.at[1 - k], core_r.at[1])

    def block_of(channel_group):
        return channel_group % 2, lax.rem(channel_group // 2 - h + HALF, HALF)

    gains = jnp.concatenate([gain_all[block_of(g)] for g in range(CHAN)], axis=0)
    for f in range(8):
        values = jnp.concatenate(
            [
                x_all[block_of(g)].astype(jnp.float32)[GROUP * f : GROUP * f + GROUP]
                for g in range(CHAN)
            ],
            axis=0,
        )
        _, normed = norm_of(values, gains)
        turned = jnp.transpose(normed * sigmoid(normed))
        hidden[WIDTH * f : WIDTH * (f + 1), :] = turned.astype(jnp.bfloat16)

    lane = lax.broadcasted_iota(jnp.int32, (BLOCK, WIDTH), 1)

    def stack_step(d):
        three = [beside[0, d], adj[d], beside[1, d]]
        three = [v.astype(jnp.float32) for v in three]
        filler = jnp.zeros((KBLOCK - 3 * SLAB, WIDTH), jnp.float32)
        for col in range(3):
            if col == 0:
                moved = [
                    jnp.where(lane == WIDTH - 1, 0.0, pltpu.roll(v, WIDTH - 1, 1)) for v in three
                ]
            elif col == 1:
                moved = three
            else:
                moved = [jnp.where(lane == 0, 0.0, pltpu.roll(v, 1, 1)) for v in three]
            for f in range(8):
                slab = jnp.concatenate(
                    [
                        moved[b][GROUP * (f + 2 - a) : GROUP * (f + 3 - a)]
                        for a in range(3)
                        for b in range(3)
                    ]
                    + [filler],
                    axis=0,
                )
                stack[d, KBLOCK * col : KBLOCK * (col + 1), WIDTH * f : WIDTH * (f + 1)] = (
                    slab.astype(jnp.bfloat16)
                )

    def grad_step(d):
        sums = jnp.dot(stack[d], hidden[...], preferred_element_type=jnp.float32)
        grad[d, :LOW, :] = sums[:, :WIDTH].astype(jnp.bfloat16)
        for col in range(3):
            begin = LOW + KBLOCK // 2 * col
            low = sums[KBLOCK * col : KBLOCK * (col + 1), WIDTH:]
            grad[d, begin : begin + KBLOCK // 2, :] = pair_lanes(low).astype(jnp.bfloat16)
        grad[d, PACK - 16 :, :] = jnp.zeros((16, WIDTH), jnp.bfloat16)
        grad_in[d, place] = grad[d, pl.ds(pl.multiple_of(place * SHARE, SHARE), SHARE), :]

        def grad_send(e):
            target = lax.rem(place + e, PLANE)
            rows = pl.ds(pl.multiple_of(target * SHARE, SHARE), SHARE)
            send(
                grad.at[d, rows],
                grad_in.at[d, place],
                grad_s,
                grad_r.at[d],
                {"rows": target * 2 + z_low},
            )

        loop(1, PLANE, grad_send)

    def turn_weights(d):
        blocks = []
        for col in range(3):
            top = w_all[d, KBLOCK * col : KBLOCK * (col + 1), :].astype(jnp.float32)
            begin = LOW + KBLOCK // 2 * col
            low = w_all[d, begin : begin + KBLOCK // 2, :].astype(jnp.float32)
            low = jnp.concatenate([low, pltpu.roll(low, 64, 1)], axis=0)
            blocks.append((top, low))
        top = jnp.transpose(jnp.concatenate([b[0] for b in blocks], axis=0))
        low = jnp.transpose(jnp.concatenate([b[1] for b in blocks], axis=0))
        w_turned[d, :WIDTH, :] = top.astype(jnp.bfloat16)
        w_turned[d, WIDTH:, :] = low[:64].astype(jnp.bfloat16)

    def part_step(p):
        pixels = pl.ds(pl.multiple_of(p * 256, 256), 256)
        total = None
        for d in range(HALF):
            term = jnp.dot(w_turned[d], stack[d, :, pixels], preferred_element_type=jnp.float32)
            total = term if total is None else total + term
        part[2 * p] = total[:, :WIDTH]
        part[2 * p + 1] = total[:, WIDTH:]

    beside_wait(0)
    stack_step(0)
    grad_step(0)
    for d in (1, 3, 2):
        drain(adj.at[d], a_r.at[d])
        beside_send(d)
    turn_weights(0)
    for d in (1, 3, 2):
        beside_wait(d)
        stack_step(d)
        grad_step(d)
    drain(w_all.at[pl.ds(1, HALF - 1), pl.ds(0, 3 * SLICE)], w_r.at[2])
    loop(1, HALF, turn_weights)
    loop(2 * (1 - k), 2 * (1 - k) + 2, part_step)
    send(part.at[pl.ds(4 * (1 - k), 4)], part_in, part_s, part_r, other)
    loop(2 * k, 2 * k + 2, part_step)

    def reduce_step(d):
        drain(grad_in.at[d, pl.ds(0, PLANE - 1)], grad_r.at[d])

        def add_step(i, total):
            return total + grad_in[d, i].astype(jnp.float32)

        red[d] = lax.fori_loop(0, PLANE, add_step, jnp.zeros((SHARE, WIDTH), jnp.float32))

    reduce_step(0)
    mine = [
        x_all[block_of(g) + (pl.ds(pl.multiple_of(k * 96, 32), 96),)].astype(jnp.float32)
        for g in range(CHAN)
    ]
    drain(part_in, part_r)
    results = []
    for f in range(4):
        values = jnp.concatenate([m[GROUP * f : GROUP * f + GROUP] for m in mine], axis=0)
        scale, normed = norm_of(values, gains)
        s = sigmoid(normed)
        adjoint = part[4 * k + f] + part_in[f]
        normed_adjoint = adjoint * s * (1.0 + normed * (1.0 - s)) * gains
        projection = jnp.sum(normed_adjoint * values, axis=0, keepdims=True)
        results.append(
            scale * normed_adjoint - values * (scale * scale * scale * projection / CHANNELS)
        )
    for g in range(CHAN):
        rows = jnp.concatenate([y[GROUP * g : GROUP * g + GROUP] for y in results], axis=0)
        staged[g] = rows.astype(jnp.bfloat16)

    for d in (1, 3, 2):
        reduce_step(d)
    red_in[z_low * HALF] = red[0, pl.ds(pl.multiple_of(z_low * PIECE, PIECE), PIECE), :]

    def red_send(d, chip_z):
        rows = pl.ds(pl.multiple_of(chip_z * PIECE, PIECE), PIECE)
        send(
            red.at[d, rows],
            red_in.at[z_low * HALF + lax.rem(HALF - d, HALF)],
            red_s,
            red_r,
            (r - z_low + chip_z, lax.rem(c + 2 * d, CHAN)),
        )

    loop(1, HALF, lambda d: red_send(d, z_low))
    loop(0, HALF, lambda d: red_send(d, 1 - z_low))
    mine_out = pl.ds(pl.multiple_of(c * 96, 32), 96)

    def out_send(d):
        target = lax.rem(c + d, CHAN)
        send(staged.at[target], x_grad.at[mine_out], out_s, out_r, (row, target))

    @pl.when(at_home)
    def _():
        pltpu.make_async_copy(staged.at[c], x_grad.at[mine_out], out_r).start()

    @pl.when(jnp.logical_not(at_home))
    def _():
        out_send(0)

    loop(1, CHAN, out_send)

    drain(red_in.at[pl.ds(0, CHAN - 1)], red_r)
    whole = jnp.zeros((PIECE, WIDTH), jnp.float32)
    for i in range(CHAN):
        whole = whole + red_in[i]
    final[...] = (whole * float(ROWS * ROWS * WIDTH) ** (-0.5)).astype(final.dtype)

    def final_send(d):
        send(final, w_grad.at[r], fin_s, fin_r, {"rows": lax.rem(r + d, ROWS)})

    loop(1, ROWS, final_send)
    own_final = pltpu.make_async_copy(final, w_grad.at[r], local.at[3])
    own_final.start()

    drain(win.at[pl.ds(0, ROWS - 1)], win_s)
    drain(gain_all.at[k, pl.ds(1, HALF - 1)], gain_s)
    drain(x_all.at[k], core_s.at[0])
    drain(gain_all.at[k], core_s.at[1])
    drain(w_all.at[pl.ds(1, HALF - 1), pl.ds(0, SHARE)], w_s.at[0])
    drain(w_all.at[pl.ds(1, HALF - 1), pl.ds(0, 3 * SHARE)], w_s.at[1])
    drain(w_all.at[pl.ds(1, HALF - 1), pl.ds(0, 3 * SLICE)], w_s.at[2])
    drain(adj.at[pl.ds(1, HALF - 1)], a_s)

    @pl.when(has_after)
    def _():
        drain(adj, after_s)

    @pl.when(has_before)
    def _():
        drain(adj, before_s)

    drain(grad_in.at[:, pl.ds(0, PLANE - 1)], grad_s)
    drain(part_in, part_s)

    @pl.when(at_home)
    def _():
        drain(x_all.at[k, pl.ds(1, HALF - 1)], x_s)
        drain(staged.at[pl.ds(0, CHAN - 1)], out_s)

    @pl.when(jnp.logical_not(at_home))
    def _():
        drain(x_all.at[k], x_s)
        drain(staged, out_s)

    drain(red_in.at[pl.ds(0, CHAN - 1)], red_s)
    drain(w_grad.at[pl.ds(0, ROWS - 1)], fin_s)
    own_final.wait()
    drain(x_grad, out_r)
    drain(w_grad.at[pl.ds(0, ROWS - 1)], fin_r)


def backward(slot, gain, frames, x, w):
    anywhere = pl.BlockSpec(memory_space=pl.ANY)
    scalars = pl.BlockSpec(memory_space=pltpu.SMEM)
    bf16, f32 = jnp.bfloat16, jnp.float32
    one = pltpu.SemaphoreType.DMA
    many = lambda n: pltpu.SemaphoreType.DMA((n,))
    return pl.pallas_call(
        kernel,
        out_shape=(
            jax.ShapeDtypeStruct((ROWS * GROUP, WIDTH), bf16),
            jax.ShapeDtypeStruct((ROWS, PIECE, WIDTH), bf16),
        ),
        in_specs=[scalars, scalars] + [anywhere] * 3,
        out_specs=(anywhere, anywhere),
        scratch_shapes=[
            pltpu.VMEM(frames.shape, bf16),
            pltpu.VMEM(x.shape, bf16),
            pltpu.VMEM(w.shape, bf16),
            pltpu.VMEM((GROUP * ROWS, WIDTH), f32),
            pltpu.SMEM((ROWS,), jnp.int32),
            pltpu.VMEM((ROWS, PADDED, WIDTH), bf16),
            pltpu.VMEM((ROWS, PADDED, WIDTH), bf16),
            pltpu.VMEM((34 * GROUP, WIDTH), bf16),
            pltpu.VMEM((HALF, BLOCK, WIDTH), bf16),
            pltpu.VMEM((2, HALF, BLOCK, WIDTH), bf16),
            pltpu.VMEM((2, HALF, 8 * GROUP, WIDTH), bf16),
            pltpu.VMEM((2, HALF, GROUP, WIDTH), f32),
            pltpu.VMEM((HALF, PACK, WIDTH), bf16),
            pltpu.VMEM((HALF, CHANNELS, LOW), bf16),
            pltpu.VMEM((HALF, LOW, 8 * WIDTH), bf16),
            pltpu.VMEM((8 * WIDTH, CHANNELS), bf16),
            pltpu.VMEM((8, CHANNELS, WIDTH), f32),
            pltpu.VMEM((4, CHANNELS, WIDTH), f32),
            pltpu.VMEM((HALF, PACK, WIDTH), bf16),
            pltpu.VMEM((HALF, PLANE, SHARE, WIDTH), bf16),
            pltpu.VMEM((CHAN, 4 * GROUP, WIDTH), bf16),
            pltpu.VMEM((HALF, SHARE, WIDTH), f32),
            pltpu.VMEM((CHAN, PIECE, WIDTH), f32),
            pltpu.VMEM((PIECE, WIDTH), bf16),
            one, one, one, one, one, one,
            many(2), many(2),
            many(3), many(3),
            one, many(HALF),
            one, one, pltpu.SemaphoreType.DMA((2, HALF)),
            one, many(HALF),
            one, one, one, one, one, one, one, one,
            many(4),
        ],
        compiler_params=pltpu.CompilerParams(
            collective_id=0, has_side_effects=True, vmem_limit_bytes=VMEM_LIMIT
        ),
    )(slot, gain, frames, x, w)


def unpack_kernel(x_in, w_in, x_out, w_out, held_x, held_w, sems):
    x_copy = pltpu.make_async_copy(x_in, held_x, sems.at[0])
    w_copy = pltpu.make_async_copy(w_in, held_w, sems.at[1])
    w_copy.start()
    x_copy.start()
    x_copy.wait()
    x_back = pltpu.make_async_copy(held_x, x_out, sems.at[2])
    x_back.start()
    w_copy.wait()
    for col in range(3):
        low = held_w[LOW + KBLOCK // 2 * col : LOW + KBLOCK // 2 * (col + 1), :]
        low = low.astype(jnp.float32)
        low = jnp.concatenate([low, pltpu.roll(low, 64, 1)], axis=0)
        top = held_w[KBLOCK * col : KBLOCK * (col + 1), :].astype(jnp.float32)
        for a in range(3):
            for b in range(3):
                begin = SLAB * a + GROUP * b
                w_out[9 * a + 3 * b + col, :, :WIDTH] = top[begin : begin + GROUP]
                w_out[9 * a + 3 * b + col, :, WIDTH:] = low[begin : begin + GROUP, :64]
    x_back.wait()


def unpack(x, w):
    anywhere = pl.BlockSpec(memory_space=pl.ANY)
    return pl.pallas_call(
        unpack_kernel,
        out_shape=(
            jax.ShapeDtypeStruct((ROWS * GROUP, WIDTH), jnp.bfloat16),
            jax.ShapeDtypeStruct((TAPS, GROUP, CHANNELS), jnp.float32),
        ),
        in_specs=[anywhere] * 2,
        out_specs=(anywhere, pl.BlockSpec(memory_space=pltpu.VMEM)),
        scratch_shapes=[
            pltpu.VMEM(x.shape, x.dtype),
            pltpu.VMEM(w.shape, w.dtype),
            pltpu.SemaphoreType.DMA((3,)),
        ],
        compiler_params=pltpu.CompilerParams(vmem_limit_bytes=VMEM_LIMIT),
    )(x, w)


def shards(frame_adjoint, frame_slot, inputs, gain, weight):
    frames = frame_adjoint.reshape(GROUP * ROWS, WIDTH)
    values = inputs.reshape(ROWS * GROUP, WIDTH)
    x_grad, w_grad = backward(frame_slot, gain, frames, values, weight)
    input_adjoint, weight_adjoint = unpack(x_grad, w_grad.reshape(PACK, WIDTH))
    return input_adjoint.reshape(ROWS, GROUP, 1, WIDTH), weight_adjoint


def solution(mesh):
    in_specs = (
        P("rows", "chan", None, None),
        P(),
        P(None, "chan", "rows", None),
        P("chan"),
        P(None, "chan", None),
    )
    out_specs = (P(None, "chan", "rows", None), P(None, "chan", None))
    return jax.shard_map(shards, mesh=mesh, in_specs=in_specs, out_specs=out_specs, check_vma=False)
```

```python
import jax
import jax.numpy as jnp
from jax import lax
from jax.experimental import pallas as pl
from jax.experimental.pallas import tpu as pltpu
from jax.sharding import PartitionSpec as P

CHANNELS = 192
GROUP = 24
WIDTH = 128
ROWS = 32
CHAN = 8
HALF = 4
RING = 4
PLANE = 16
TAPS = 27
PADDED = 32
FRAMES = 10
BLOCK = FRAMES * GROUP
SLAB = 72
KBLOCK = 224
PACK = 1024
LOW = 3 * KBLOCK
PIECE = PACK // ROWS
SLICE = PACK // RING
SHARE = PACK // PLANE
EPSILON = 1e-06
MESH = pl.DeviceIdType.MESH
VMEM_LIMIT = 56 * 1024 * 1024


def owner_of(row):
    return row + lax.rem(row % 8 // 2, 2) * (1 - 2 * lax.rem(row, 2))


def greet_all(r, c):
    barrier = pltpu.get_barrier_semaphore()

    def tell(rows_index, chan_index):
        pl.semaphore_signal(
            barrier, inc=1, device_id=(rows_index, chan_index), device_id_type=MESH
        )

    def chan_step(d):
        chan_index = lax.rem(c + d, CHAN)
        tell(r, chan_index)
        tell(r + 1 - 2 * lax.rem(r, 2), chan_index)

    loop(1, ROWS, lambda d: tell(lax.rem(r + d, ROWS), c))
    loop(1, CHAN, chan_step)
    return barrier, ROWS - 1 + 2 * (CHAN - 1)


def send(src, dst, send_sem, recv_sem, device):
    pltpu.make_async_remote_copy(
        src_ref=src,
        dst_ref=dst,
        send_sem=send_sem,
        recv_sem=recv_sem,
        device_id=device,
        device_id_type=MESH,
    ).start()


def drain(ref, sem):
    pltpu.make_async_copy(ref, ref, sem).wait()


def loop(low, high, step):
    def body(i, carry):
        step(i)
        return carry

    lax.fori_loop(low, high, body, 0)


def norm_of(values, gain):
    squares = jnp.sum(values * values, axis=0, keepdims=True)
    scale = lax.rsqrt(squares / CHANNELS + EPSILON)
    return scale, values * scale * gain


def sigmoid(v):
    return 1.0 / (1.0 + jnp.exp(-v))


def pair_lanes(low):
    return jnp.concatenate([low[: KBLOCK // 2], low[KBLOCK // 2 :]], axis=1)


def kernel(
    slot,
    gain,
    frames_in,
    x_in,
    w_in,
    x_grad,
    w_grad,
    frames,
    x,
    w,
    wide,
    inverse,
    win,
    recv,
    ordered,
    adj,
    beside,
    x_all,
    gain_all,
    w_all,
    w_turned,
    stack,
    hidden,
    part,
    part_in,
    grad,
    grad_in,
    staged,
    red,
    red_in,
    final,
    win_s,
    win_r,
    x_s,
    x_r,
    gain_s,
    gain_r,
    core_s,
    core_r,
    w_s,
    w_r,
    a_s,
    a_r,
    after_s,
    before_s,
    beside_r,
    grad_s,
    grad_r,
    part_s,
    part_r,
    out_s,
    out_r,
    red_s,
    red_r,
    fin_s,
    fin_r,
    local,
):
    r = lax.axis_index("rows")
    c = lax.axis_index("chan")
    h = c // 2
    k = lax.rem(c, 2)
    z_low = lax.rem(r, 2)
    place = r // 2
    chip_x = r // 8
    row = owner_of(r)
    at_home = row == r
    other = {"chan": c + 1 - 2 * k}

    fetches = [
        pltpu.make_async_copy(src, dst, local.at[i])
        for i, (src, dst) in enumerate(((frames_in, frames), (w_in, w), (x_in, x)))
    ]
    for fetch in fetches:
        fetch.start()
    barrier, greetings = greet_all(r, c)
    fetches[0].wait()

    wide[...] = frames[...].astype(jnp.float32)
    empty = jnp.zeros((PADDED - GROUP, WIDTH), jnp.float32)

    def win_build(i):
        rows = wide[pl.ds(i, GROUP, stride=ROWS), :]
        win[owner_of(i)] = jnp.concatenate([rows, empty], axis=0).astype(jnp.bfloat16)

    loop(0, ROWS, win_build)
    recv[r] = win[r]
    gain_all[k, 0] = jnp.concatenate(
        [jnp.full((1, WIDTH), gain[j], jnp.float32) for j in range(GROUP)], axis=0
    )
    ordered[pl.ds(32 * GROUP, 2 * GROUP), :] = jnp.zeros((2 * GROUP, WIDTH), jnp.bfloat16)

    fetches[1].wait()
    for col in range(3):
        rows = [w[9 * a + 3 * b + col].astype(jnp.float32) for a in range(3) for b in range(3)]
        rows = jnp.concatenate(
            rows + [jnp.zeros((KBLOCK - 3 * SLAB, CHANNELS), jnp.float32)], axis=0
        )
        w_all[0, KBLOCK * col : KBLOCK * (col + 1), :] = rows[:, :WIDTH].astype(jnp.bfloat16)
        begin = LOW + KBLOCK // 2 * col
        w_all[0, begin : begin + KBLOCK // 2, :] = pair_lanes(rows[:, WIDTH:]).astype(jnp.bfloat16)
    w_all[0, PACK - 16 :, :] = jnp.zeros((16, WIDTH), jnp.bfloat16)
    fetches[2].wait()

    pl.semaphore_wait(barrier, greetings)

    mine_w = pl.ds(pl.multiple_of(SHARE * place, SHARE), SHARE)

    def w_send(d):
        target = lax.rem(c + 2 * d, CHAN)
        send(w_all.at[0, mine_w], w_all.at[HALF - d, mine_w], w_s.at[0], w_r.at[0], {"chan": target})

    def w_spread(e):
        block = w_all.at[pl.ds(1, HALF - 1), mine_w]
        target = lax.rem(place + e, PLANE) * 2 + z_low
        send(block, block, w_s.at[1], w_r.at[1], {"rows": target})

    def win_send(d):
        target = lax.rem(r + d, ROWS)
        send(win.at[target], recv.at[r], win_s, win_r, {"rows": target})

    loop(1, HALF, w_send)
    loop(1, ROWS, win_send)

    def x_send(d):
        target = lax.rem(c + 2 * d, CHAN)
        begin = pl.multiple_of((target // 2) * 192, 64)
        send(
            x.at[pl.ds(begin, 192)],
            x_all.at[k, lax.rem(HALF - d, HALF)],
            x_s,
            x_r,
            (row, target),
        )

    def gain_send(d):
        target = lax.rem(c + 2 * d, CHAN)
        send(gain_all.at[k, 0], gain_all.at[k, HALF - d], gain_s, gain_r, {"chan": target})

    @pl.when(at_home)
    def _():
        begin = pl.multiple_of(h * 192, 64)
        pltpu.make_async_copy(x.at[pl.ds(begin, 192)], x_all.at[k, 0], x_r).start()

    @pl.when(jnp.logical_not(at_home))
    def _():
        x_send(0)

    loop(1, HALF, x_send)
    loop(1, HALF, gain_send)

    def invert(t):
        found = jnp.int32(0)
        for j in range(ROWS):
            found = jnp.where(slot[j] == t, j, found)
        inverse[t] = found

    loop(0, ROWS, invert)
    drain(w_all.at[pl.ds(1, HALF - 1), pl.ds(0, SHARE)], w_r.at[0])
    loop(1, PLANE, w_spread)
    drain(recv.at[pl.ds(0, ROWS - 1)], win_r)

    def order_step(p):
        low = recv[inverse[2 * p]].astype(jnp.float32)[:GROUP]
        high = recv[inverse[2 * p + 1]].astype(jnp.float32)[:GROUP]
        both = jnp.concatenate([low, high], axis=0).astype(jnp.bfloat16)
        ordered[pl.ds(pl.multiple_of(p * 2 * GROUP, 2 * GROUP), 2 * GROUP), :] = both

    loop(0, ROWS // 2, order_step)

    def a_send(d):
        target = lax.rem(c + 2 * d, CHAN)
        start = pl.multiple_of((target // 2) * (8 * GROUP), 64)
        send(
            ordered.at[pl.ds(start, BLOCK)],
            adj.at[HALF - d],
            a_s,
            a_r.at[HALF - d],
            {"chan": target},
        )

    for d in (1, 3):
        a_send(d)
    adj[0] = ordered[pl.ds(pl.multiple_of(h * (8 * GROUP), 64), BLOCK), :]
    has_after = row < ROWS - 1
    has_before = row > 0

    @pl.when(jnp.logical_not(has_after))
    def _():
        beside[0] = jnp.zeros((HALF, BLOCK, WIDTH), jnp.bfloat16)

    @pl.when(jnp.logical_not(has_before))
    def _():
        beside[1] = jnp.zeros((HALF, BLOCK, WIDTH), jnp.bfloat16)

    def beside_send(d):
        @pl.when(has_after)
        def _():
            target = {"rows": owner_of(row + 1)}
            send(adj.at[d], beside.at[1, d], after_s, beside_r.at[1, d], target)

        @pl.when(has_before)
        def _():
            target = {"rows": owner_of(row - 1)}
            send(adj.at[d], beside.at[0, d], before_s, beside_r.at[0, d], target)

    def beside_wait(d):
        @pl.when(has_after)
        def _():
            drain(beside.at[0, d], beside_r.at[0, d])

        @pl.when(has_before)
        def _():
            drain(beside.at[1, d], beside_r.at[1, d])

    beside_send(0)

    drain(x_all.at[k], x_r)
    drain(gain_all.at[k, pl.ds(1, HALF - 1)], gain_r)
    send(x_all.at[k], x_all.at[k], core_s.at[0], core_r.at[0], other)
    send(gain_all.at[k], gain_all.at[k], core_s.at[1], core_r.at[1], other)

    a_send(2)
    drain(x_all.at[1 - k], core_r.at[0])
    drain(gain_all.at[1 - k], core_r.at[1])

    def block_of(channel_group):
        return channel_group % 2, lax.rem(channel_group // 2 - h + HALF, HALF)

    gains = jnp.concatenate([gain_all[block_of(g)] for g in range(CHAN)], axis=0)
    for f in range(8):
        values = jnp.concatenate(
            [
                x_all[block_of(g)].astype(jnp.float32)[GROUP * f : GROUP * f + GROUP]
                for g in range(CHAN)
            ],
            axis=0,
        )
        _, normed = norm_of(values, gains)
        turned = jnp.transpose(normed * sigmoid(normed))
        hidden[WIDTH * f : WIDTH * (f + 1), :] = turned.astype(jnp.bfloat16)

    lane = lax.broadcasted_iota(jnp.int32, (BLOCK, WIDTH), 1)

    def stack_step(d):
        three = [beside[0, d], adj[d], beside[1, d]]
        three = [v.astype(jnp.float32) for v in three]
        filler = jnp.zeros((KBLOCK - 3 * SLAB, WIDTH), jnp.float32)
        for col in range(3):
            if col == 0:
                moved = [
                    jnp.where(lane == WIDTH - 1, 0.0, pltpu.roll(v, WIDTH - 1, 1)) for v in three
                ]
            elif col == 1:
                moved = three
            else:
                moved = [jnp.where(lane == 0, 0.0, pltpu.roll(v, 1, 1)) for v in three]
            for f in range(8):
                slab = jnp.concatenate(
                    [
                        moved[b][GROUP * (f + 2 - a) : GROUP * (f + 3 - a)]
                        for a in range(3)
                        for b in range(3)
                    ]
                    + [filler],
                    axis=0,
                )
                stack[d, KBLOCK * col : KBLOCK * (col + 1), WIDTH * f : WIDTH * (f + 1)] = (
                    slab.astype(jnp.bfloat16)
                )

    def grad_step(d):
        sums = jnp.dot(stack[d], hidden[...], preferred_element_type=jnp.float32)
        grad[d, :LOW, :] = sums[:, :WIDTH].astype(jnp.bfloat16)
        for col in range(3):
            begin = LOW + KBLOCK // 2 * col
            low = sums[KBLOCK * col : KBLOCK * (col + 1), WIDTH:]
            grad[d, begin : begin + KBLOCK // 2, :] = pair_lanes(low).astype(jnp.bfloat16)
        grad[d, PACK - 16 :, :] = jnp.zeros((16, WIDTH), jnp.bfloat16)
        grad_in[d, place] = grad[d, pl.ds(pl.multiple_of(place * SHARE, SHARE), SHARE), :]

        def grad_send(e):
            target = lax.rem(place + e, PLANE)
            rows = pl.ds(pl.multiple_of(target * SHARE, SHARE), SHARE)
            send(
                grad.at[d, rows],
                grad_in.at[d, place],
                grad_s,
                grad_r.at[d],
                {"rows": target * 2 + z_low},
            )

        loop(1, PLANE, grad_send)

    def turn_weights(d):
        blocks = []
        for col in range(3):
            top = w_all[d, KBLOCK * col : KBLOCK * (col + 1), :].astype(jnp.float32)
            begin = LOW + KBLOCK // 2 * col
            low = w_all[d, begin : begin + KBLOCK // 2, :].astype(jnp.float32)
            low = jnp.concatenate([low, pltpu.roll(low, 64, 1)], axis=0)
            blocks.append((top, low))
        top = jnp.transpose(jnp.concatenate([b[0] for b in blocks], axis=0))
        low = jnp.transpose(jnp.concatenate([b[1] for b in blocks], axis=0))
        w_turned[d, :WIDTH, :] = top.astype(jnp.bfloat16)
        w_turned[d, WIDTH:, :] = low[:64].astype(jnp.bfloat16)

    def part_step(p):
        pixels = pl.ds(pl.multiple_of(p * 256, 256), 256)
        total = None
        for d in range(HALF):
            term = jnp.dot(w_turned[d], stack[d, :, pixels], preferred_element_type=jnp.float32)
            total = term if total is None else total + term
        part[2 * p] = total[:, :WIDTH]
        part[2 * p + 1] = total[:, WIDTH:]

    for d in (1, 3):
        drain(adj.at[d], a_r.at[d])
        beside_send(d)
    beside_wait(0)
    stack_step(0)
    grad_step(0)
    drain(adj.at[2], a_r.at[2])
    beside_send(2)
    turn_weights(0)
    for d in (1, 3, 2):
        beside_wait(d)
        stack_step(d)
        grad_step(d)
    drain(w_all.at[pl.ds(1, HALF - 1), pl.ds(0, 15 * SHARE)], w_r.at[1])
    loop(1, HALF, turn_weights)
    loop(2 * (1 - k), 2 * (1 - k) + 2, part_step)
    send(part.at[pl.ds(4 * (1 - k), 4)], part_in, part_s, part_r, other)
    loop(2 * k, 2 * k + 2, part_step)

    def red_send(d, chip_z):
        rows = pl.ds(pl.multiple_of(chip_z * PIECE, PIECE), PIECE)
        send(
            red.at[d, rows],
            red_in.at[z_low * HALF + lax.rem(HALF - d, HALF)],
            red_s,
            red_r,
            (r - z_low + chip_z, lax.rem(c + 2 * d, CHAN)),
        )

    def reduce_step(d):
        drain(grad_in.at[d, pl.ds(0, PLANE - 1)], grad_r.at[d])

        def add_step(i, total):
            return total + grad_in[d, i].astype(jnp.float32)

        red[d] = lax.fori_loop(0, PLANE, add_step, jnp.zeros((SHARE, WIDTH), jnp.float32))
        red_send(d, 1 - z_low)
        if d > 0:
            red_send(d, z_low)

    reduce_step(0)
    mine = [
        x_all[block_of(g) + (pl.ds(pl.multiple_of(k * 96, 32), 96),)].astype(jnp.float32)
        for g in range(CHAN)
    ]
    drain(part_in, part_r)
    results = []
    for f in range(4):
        values = jnp.concatenate([m[GROUP * f : GROUP * f + GROUP] for m in mine], axis=0)
        scale, normed = norm_of(values, gains)
        s = sigmoid(normed)
        adjoint = part[4 * k + f] + part_in[f]
        normed_adjoint = adjoint * s * (1.0 + normed * (1.0 - s)) * gains
        projection = jnp.sum(normed_adjoint * values, axis=0, keepdims=True)
        results.append(
            scale * normed_adjoint - values * (scale * scale * scale * projection / CHANNELS)
        )
    for g in range(CHAN):
        rows = jnp.concatenate([y[GROUP * g : GROUP * g + GROUP] for y in results], axis=0)
        staged[g] = rows.astype(jnp.bfloat16)

    for d in (1, 3, 2):
        reduce_step(d)
    red_in[z_low * HALF] = red[0, pl.ds(pl.multiple_of(z_low * PIECE, PIECE), PIECE), :]

    mine_out = pl.ds(pl.multiple_of(c * 96, 32), 96)

    def out_send(d):
        target = lax.rem(c + d, CHAN)
        send(staged.at[target], x_grad.at[mine_out], out_s, out_r, (row, target))

    @pl.when(at_home)
    def _():
        pltpu.make_async_copy(staged.at[c], x_grad.at[mine_out], out_r).start()

    @pl.when(jnp.logical_not(at_home))
    def _():
        out_send(0)

    loop(1, CHAN, out_send)

    drain(red_in.at[pl.ds(0, CHAN - 1)], red_r)
    whole = jnp.zeros((PIECE, WIDTH), jnp.float32)
    for i in range(CHAN):
        whole = whole + red_in[i]
    final[...] = (whole * float(ROWS * ROWS * WIDTH) ** (-0.5)).astype(final.dtype)

    def final_send(d):
        send(final, w_grad.at[r], fin_s, fin_r, {"rows": lax.rem(r + d, ROWS)})

    loop(1, ROWS, final_send)
    own_final = pltpu.make_async_copy(final, w_grad.at[r], local.at[3])
    own_final.start()

    drain(win.at[pl.ds(0, ROWS - 1)], win_s)
    drain(gain_all.at[k, pl.ds(1, HALF - 1)], gain_s)
    drain(x_all.at[k], core_s.at[0])
    drain(gain_all.at[k], core_s.at[1])
    drain(w_all.at[pl.ds(1, HALF - 1), pl.ds(0, SHARE)], w_s.at[0])
    drain(w_all.at[pl.ds(1, HALF - 1), pl.ds(0, 15 * SHARE)], w_s.at[1])
    drain(adj.at[pl.ds(1, HALF - 1)], a_s)

    @pl.when(has_after)
    def _():
        drain(adj, after_s)

    @pl.when(has_before)
    def _():
        drain(adj, before_s)

    drain(grad_in.at[:, pl.ds(0, PLANE - 1)], grad_s)
    drain(part_in, part_s)

    @pl.when(at_home)
    def _():
        drain(x_all.at[k, pl.ds(1, HALF - 1)], x_s)
        drain(staged.at[pl.ds(0, CHAN - 1)], out_s)

    @pl.when(jnp.logical_not(at_home))
    def _():
        drain(x_all.at[k], x_s)
        drain(staged, out_s)

    drain(red_in.at[pl.ds(0, CHAN - 1)], red_s)
    drain(w_grad.at[pl.ds(0, ROWS - 1)], fin_s)
    own_final.wait()
    drain(x_grad, out_r)
    drain(w_grad.at[pl.ds(0, ROWS - 1)], fin_r)


def backward(slot, gain, frames, x, w):
    anywhere = pl.BlockSpec(memory_space=pl.ANY)
    scalars = pl.BlockSpec(memory_space=pltpu.SMEM)
    bf16, f32 = jnp.bfloat16, jnp.float32
    one = pltpu.SemaphoreType.DMA
    many = lambda n: pltpu.SemaphoreType.DMA((n,))
    return pl.pallas_call(
        kernel,
        out_shape=(
            jax.ShapeDtypeStruct((ROWS * GROUP, WIDTH), bf16),
            jax.ShapeDtypeStruct((ROWS, PIECE, WIDTH), bf16),
        ),
        in_specs=[scalars, scalars] + [anywhere] * 3,
        out_specs=(anywhere, anywhere),
        scratch_shapes=[
            pltpu.VMEM(frames.shape, bf16),
            pltpu.VMEM(x.shape, bf16),
            pltpu.VMEM(w.shape, bf16),
            pltpu.VMEM((GROUP * ROWS, WIDTH), f32),
            pltpu.SMEM((ROWS,), jnp.int32),
            pltpu.VMEM((ROWS, PADDED, WIDTH), bf16),
            pltpu.VMEM((ROWS, PADDED, WIDTH), bf16),
            pltpu.VMEM((34 * GROUP, WIDTH), bf16),
            pltpu.VMEM((HALF, BLOCK, WIDTH), bf16),
            pltpu.VMEM((2, HALF, BLOCK, WIDTH), bf16),
            pltpu.VMEM((2, HALF, 8 * GROUP, WIDTH), bf16),
            pltpu.VMEM((2, HALF, GROUP, WIDTH), f32),
            pltpu.VMEM((HALF, PACK, WIDTH), bf16),
            pltpu.VMEM((HALF, CHANNELS, LOW), bf16),
            pltpu.VMEM((HALF, LOW, 8 * WIDTH), bf16),
            pltpu.VMEM((8 * WIDTH, CHANNELS), bf16),
            pltpu.VMEM((8, CHANNELS, WIDTH), f32),
            pltpu.VMEM((4, CHANNELS, WIDTH), f32),
            pltpu.VMEM((HALF, PACK, WIDTH), bf16),
            pltpu.VMEM((HALF, PLANE, SHARE, WIDTH), bf16),
            pltpu.VMEM((CHAN, 4 * GROUP, WIDTH), bf16),
            pltpu.VMEM((HALF, SHARE, WIDTH), f32),
            pltpu.VMEM((CHAN, PIECE, WIDTH), f32),
            pltpu.VMEM((PIECE, WIDTH), bf16),
            one, one, one, one, one, one,
            many(2), many(2),
            many(2), many(2),
            one, many(HALF),
            one, one, pltpu.SemaphoreType.DMA((2, HALF)),
            one, many(HALF),
            one, one, one, one, one, one, one, one,
            many(4),
        ],
        compiler_params=pltpu.CompilerParams(
            collective_id=0, has_side_effects=True, vmem_limit_bytes=VMEM_LIMIT
        ),
    )(slot, gain, frames, x, w)


def unpack_kernel(x_in, w_in, x_out, w_out, held_x, held_w, sems):
    x_copy = pltpu.make_async_copy(x_in, held_x, sems.at[0])
    w_copy = pltpu.make_async_copy(w_in, held_w, sems.at[1])
    w_copy.start()
    x_copy.start()
    x_copy.wait()
    x_back = pltpu.make_async_copy(held_x, x_out, sems.at[2])
    x_back.start()
    w_copy.wait()
    for col in range(3):
        low = held_w[LOW + KBLOCK // 2 * col : LOW + KBLOCK // 2 * (col + 1), :]
        low = low.astype(jnp.float32)
        low = jnp.concatenate([low, pltpu.roll(low, 64, 1)], axis=0)
        top = held_w[KBLOCK * col : KBLOCK * (col + 1), :].astype(jnp.float32)
        for a in range(3):
            for b in range(3):
                begin = SLAB * a + GROUP * b
                w_out[9 * a + 3 * b + col, :, :WIDTH] = top[begin : begin + GROUP]
                w_out[9 * a + 3 * b + col, :, WIDTH:] = low[begin : begin + GROUP, :64]
    x_back.wait()


def unpack(x, w):
    anywhere = pl.BlockSpec(memory_space=pl.ANY)
    return pl.pallas_call(
        unpack_kernel,
        out_shape=(
            jax.ShapeDtypeStruct((ROWS * GROUP, WIDTH), jnp.bfloat16),
            jax.ShapeDtypeStruct((TAPS, GROUP, CHANNELS), jnp.float32),
        ),
        in_specs=[anywhere] * 2,
        out_specs=(anywhere, pl.BlockSpec(memory_space=pltpu.VMEM)),
        scratch_shapes=[
            pltpu.VMEM(x.shape, x.dtype),
            pltpu.VMEM(w.shape, w.dtype),
            pltpu.SemaphoreType.DMA((3,)),
        ],
        compiler_params=pltpu.CompilerParams(vmem_limit_bytes=VMEM_LIMIT),
    )(x, w)


def shards(frame_adjoint, frame_slot, inputs, gain, weight):
    frames = frame_adjoint.reshape(GROUP * ROWS, WIDTH)
    values = inputs.reshape(ROWS * GROUP, WIDTH)
    x_grad, w_grad = backward(frame_slot, gain, frames, values, weight)
    input_adjoint, weight_adjoint = unpack(x_grad, w_grad.reshape(PACK, WIDTH))
    return input_adjoint.reshape(ROWS, GROUP, 1, WIDTH), weight_adjoint


def solution(mesh):
    in_specs = (
        P("rows", "chan", None, None),
        P(),
        P(None, "chan", "rows", None),
        P("chan"),
        P(None, "chan", None),
    )
    out_specs = (P(None, "chan", "rows", None), P(None, "chan", None))
    return jax.shard_map(shards, mesh=mesh, in_specs=in_specs, out_specs=out_specs, check_vma=False)
```

```python
import jax
import jax.numpy as jnp
from jax import lax
from jax.experimental import pallas as pl
from jax.experimental.pallas import tpu as pltpu
from jax.sharding import PartitionSpec as P

CHANNELS = 192
GROUP = 24
WIDTH = 128
ROWS = 32
CHAN = 8
HALF = 4
RING = 4
PLANE = 16
TAPS = 27
PADDED = 32
FRAMES = 10
BLOCK = FRAMES * GROUP
SLAB = 72
KBLOCK = 224
PACK = 1024
LOW = 3 * KBLOCK
PIECE = PACK // ROWS
SLICE = PACK // RING
SHARE = PACK // PLANE
EPSILON = 1e-06
MESH = pl.DeviceIdType.MESH
VMEM_LIMIT = 56 * 1024 * 1024


def owner_of(row):
    return row + lax.rem(row % 8 // 2, 2) * (1 - 2 * lax.rem(row, 2))


def greet_all(r, c):
    barrier = pltpu.get_barrier_semaphore()

    def tell(rows_index, chan_index):
        pl.semaphore_signal(
            barrier, inc=1, device_id=(rows_index, chan_index), device_id_type=MESH
        )

    def chan_step(d):
        chan_index = lax.rem(c + d, CHAN)
        tell(r, chan_index)
        tell(r + 1 - 2 * lax.rem(r, 2), chan_index)

    loop(1, ROWS, lambda d: tell(lax.rem(r + d, ROWS), c))
    loop(1, CHAN, chan_step)
    return barrier, ROWS - 1 + 2 * (CHAN - 1)


def send(src, dst, send_sem, recv_sem, device):
    pltpu.make_async_remote_copy(
        src_ref=src,
        dst_ref=dst,
        send_sem=send_sem,
        recv_sem=recv_sem,
        device_id=device,
        device_id_type=MESH,
    ).start()


def drain(ref, sem):
    pltpu.make_async_copy(ref, ref, sem).wait()


def loop(low, high, step):
    def body(i, carry):
        step(i)
        return carry

    lax.fori_loop(low, high, body, 0)


def norm_of(values, gain):
    squares = jnp.sum(values * values, axis=0, keepdims=True)
    scale = lax.rsqrt(squares / CHANNELS + EPSILON)
    return scale, values * scale * gain


def sigmoid(v):
    return 1.0 / (1.0 + jnp.exp(-v))


def pair_lanes(low):
    return jnp.concatenate([low[: KBLOCK // 2], low[KBLOCK // 2 :]], axis=1)


def kernel(
    slot_in,
    gain_in,
    frames_in,
    x_in,
    w_in,
    x_grad,
    w_grad,
    slot,
    gain,
    frames,
    x,
    w,
    wide,
    inverse,
    win,
    recv,
    ordered,
    adj,
    beside,
    x_all,
    gain_all,
    w_all,
    w_turned,
    stack,
    hidden,
    part,
    part_in,
    grad,
    grad_in,
    staged,
    red,
    red_in,
    final,
    win_s,
    win_r,
    x_s,
    x_r,
    gain_s,
    gain_r,
    core_s,
    core_r,
    w_s,
    w_r,
    a_s,
    a_r,
    after_s,
    before_s,
    beside_r,
    grad_s,
    grad_r,
    part_s,
    part_r,
    out_s,
    out_r,
    red_s,
    red_r,
    fin_s,
    fin_r,
    local,
):
    r = lax.axis_index("rows")
    c = lax.axis_index("chan")
    h = c // 2
    k = lax.rem(c, 2)
    z_low = lax.rem(r, 2)
    place = r // 2
    chip_x = r // 8
    row = owner_of(r)
    at_home = row == r
    other = {"chan": c + 1 - 2 * k}

    fetches = [
        pltpu.make_async_copy(src, dst, local.at[i])
        for i, (src, dst) in enumerate(
            ((frames_in, frames), (w_in, w), (x_in, x), (gain_in, gain), (slot_in, slot))
        )
    ]
    for fetch in fetches:
        fetch.start()
    barrier, greetings = greet_all(r, c)
    fetches[0].wait()

    wide[...] = frames[...].astype(jnp.float32)
    empty = jnp.zeros((PADDED - GROUP, WIDTH), jnp.float32)

    def win_build(i):
        rows = wide[pl.ds(i, GROUP, stride=ROWS), :]
        win[owner_of(i)] = jnp.concatenate([rows, empty], axis=0).astype(jnp.bfloat16)

    loop(0, ROWS, win_build)
    recv[r] = win[r]
    fetches[3].wait()
    gain_all[k, 0] = jnp.concatenate(
        [jnp.full((1, WIDTH), gain[j], jnp.float32) for j in range(GROUP)], axis=0
    )
    ordered[pl.ds(32 * GROUP, 2 * GROUP), :] = jnp.zeros((2 * GROUP, WIDTH), jnp.bfloat16)

    fetches[1].wait()
    for col in range(3):
        rows = [w[9 * a + 3 * b + col].astype(jnp.float32) for a in range(3) for b in range(3)]
        rows = jnp.concatenate(
            rows + [jnp.zeros((KBLOCK - 3 * SLAB, CHANNELS), jnp.float32)], axis=0
        )
        w_all[0, KBLOCK * col : KBLOCK * (col + 1), :] = rows[:, :WIDTH].astype(jnp.bfloat16)
        begin = LOW + KBLOCK // 2 * col
        w_all[0, begin : begin + KBLOCK // 2, :] = pair_lanes(rows[:, WIDTH:]).astype(jnp.bfloat16)
    w_all[0, PACK - 16 :, :] = jnp.zeros((16, WIDTH), jnp.bfloat16)
    fetches[2].wait()
    fetches[4].wait()

    pl.semaphore_wait(barrier, greetings)

    mine_w = pl.ds(pl.multiple_of(SHARE * place, SHARE), SHARE)

    def w_send(d):
        target = lax.rem(c + 2 * d, CHAN)
        send(w_all.at[0, mine_w], w_all.at[HALF - d, mine_w], w_s.at[0], w_r.at[0], {"chan": target})

    def w_spread(e):
        block = w_all.at[pl.ds(1, HALF - 1), mine_w]
        target = lax.rem(place + e, PLANE) * 2 + z_low
        send(block, block, w_s.at[1], w_r.at[1], {"rows": target})

    def win_send(d):
        target = lax.rem(r + d, ROWS)
        send(win.at[target], recv.at[r], win_s, win_r, {"rows": target})

    loop(1, HALF, w_send)
    loop(1, ROWS, win_send)

    def x_send(d):
        target = lax.rem(c + 2 * d, CHAN)
        begin = pl.multiple_of((target // 2) * 192, 64)
        send(
            x.at[pl.ds(begin, 192)],
            x_all.at[k, lax.rem(HALF - d, HALF)],
            x_s,
            x_r,
            (row, target),
        )

    def gain_send(d):
        target = lax.rem(c + 2 * d, CHAN)
        send(gain_all.at[k, 0], gain_all.at[k, HALF - d], gain_s, gain_r, {"chan": target})

    @pl.when(at_home)
    def _():
        begin = pl.multiple_of(h * 192, 64)
        pltpu.make_async_copy(x.at[pl.ds(begin, 192)], x_all.at[k, 0], x_r).start()

    @pl.when(jnp.logical_not(at_home))
    def _():
        x_send(0)

    loop(1, HALF, x_send)
    loop(1, HALF, gain_send)

    def invert(t):
        found = jnp.int32(0)
        for j in range(ROWS):
            found = jnp.where(slot[j] == t, j, found)
        inverse[t] = found

    loop(0, ROWS, invert)
    drain(w_all.at[pl.ds(1, HALF - 1), pl.ds(0, SHARE)], w_r.at[0])
    loop(1, PLANE, w_spread)
    drain(recv.at[pl.ds(0, ROWS - 1)], win_r)

    def order_step(p):
        low = recv[inverse[2 * p]].astype(jnp.float32)[:GROUP]
        high = recv[inverse[2 * p + 1]].astype(jnp.float32)[:GROUP]
        both = jnp.concatenate([low, high], axis=0).astype(jnp.bfloat16)
        ordered[pl.ds(pl.multiple_of(p * 2 * GROUP, 2 * GROUP), 2 * GROUP), :] = both

    loop(0, ROWS // 2, order_step)

    def a_send(d):
        target = lax.rem(c + 2 * d, CHAN)
        start = pl.multiple_of((target // 2) * (8 * GROUP), 64)
        send(
            ordered.at[pl.ds(start, BLOCK)],
            adj.at[HALF - d],
            a_s,
            a_r.at[HALF - d],
            {"chan": target},
        )

    for d in (1, 3):
        a_send(d)
    adj[0] = ordered[pl.ds(pl.multiple_of(h * (8 * GROUP), 64), BLOCK), :]
    has_after = row < ROWS - 1
    has_before = row > 0

    @pl.when(jnp.logical_not(has_after))
    def _():
        beside[0] = jnp.zeros((HALF, BLOCK, WIDTH), jnp.bfloat16)

    @pl.when(jnp.logical_not(has_before))
    def _():
        beside[1] = jnp.zeros((HALF, BLOCK, WIDTH), jnp.bfloat16)

    def beside_send(d):
        @pl.when(has_after)
        def _():
            target = {"rows": owner_of(row + 1)}
            send(adj.at[d], beside.at[1, d], after_s, beside_r.at[1, d], target)

        @pl.when(has_before)
        def _():
            target = {"rows": owner_of(row - 1)}
            send(adj.at[d], beside.at[0, d], before_s, beside_r.at[0, d], target)

    def beside_wait(d):
        @pl.when(has_after)
        def _():
            drain(beside.at[0, d], beside_r.at[0, d])

        @pl.when(has_before)
        def _():
            drain(beside.at[1, d], beside_r.at[1, d])

    beside_send(0)

    drain(x_all.at[k], x_r)
    drain(gain_all.at[k, pl.ds(1, HALF - 1)], gain_r)
    send(x_all.at[k], x_all.at[k], core_s.at[0], core_r.at[0], other)
    send(gain_all.at[k], gain_all.at[k], core_s.at[1], core_r.at[1], other)

    drain(x_all.at[1 - k], core_r.at[0])
    drain(gain_all.at[1 - k], core_r.at[1])

    def block_of(channel_group):
        return channel_group % 2, lax.rem(channel_group // 2 - h + HALF, HALF)

    gains = jnp.concatenate([gain_all[block_of(g)] for g in range(CHAN)], axis=0)
    for f in range(8):
        values = jnp.concatenate(
            [
                x_all[block_of(g)].astype(jnp.float32)[GROUP * f : GROUP * f + GROUP]
                for g in range(CHAN)
            ],
            axis=0,
        )
        _, normed = norm_of(values, gains)
        turned = jnp.transpose(normed * sigmoid(normed))
        hidden[WIDTH * f : WIDTH * (f + 1), :] = turned.astype(jnp.bfloat16)

    lane = lax.broadcasted_iota(jnp.int32, (BLOCK, WIDTH), 1)

    def stack_step(d):
        three = [beside[0, d], adj[d], beside[1, d]]
        three = [v.astype(jnp.float32) for v in three]
        filler = jnp.zeros((KBLOCK - 3 * SLAB, WIDTH), jnp.float32)
        for col in range(3):
            if col == 0:
                moved = [
                    jnp.where(lane == WIDTH - 1, 0.0, pltpu.roll(v, WIDTH - 1, 1)) for v in three
                ]
            elif col == 1:
                moved = three
            else:
                moved = [jnp.where(lane == 0, 0.0, pltpu.roll(v, 1, 1)) for v in three]
            for f in range(8):
                slab = jnp.concatenate(
                    [
                        moved[b][GROUP * (f + 2 - a) : GROUP * (f + 3 - a)]
                        for a in range(3)
                        for b in range(3)
                    ]
                    + [filler],
                    axis=0,
                )
                stack[d, KBLOCK * col : KBLOCK * (col + 1), WIDTH * f : WIDTH * (f + 1)] = (
                    slab.astype(jnp.bfloat16)
                )

    def grad_step(d):
        sums = jnp.dot(stack[d], hidden[...], preferred_element_type=jnp.float32)
        grad[d, :LOW, :] = sums[:, :WIDTH].astype(jnp.bfloat16)
        for col in range(3):
            begin = LOW + KBLOCK // 2 * col
            low = sums[KBLOCK * col : KBLOCK * (col + 1), WIDTH:]
            grad[d, begin : begin + KBLOCK // 2, :] = pair_lanes(low).astype(jnp.bfloat16)
        grad[d, PACK - 16 :, :] = jnp.zeros((16, WIDTH), jnp.bfloat16)
        grad_in[d, place] = grad[d, pl.ds(pl.multiple_of(place * SHARE, SHARE), SHARE), :]

        def grad_send(e):
            target = lax.rem(place + e, PLANE)
            rows = pl.ds(pl.multiple_of(target * SHARE, SHARE), SHARE)
            send(
                grad.at[d, rows],
                grad_in.at[d, place],
                grad_s,
                grad_r.at[d],
                {"rows": target * 2 + z_low},
            )

        loop(1, PLANE, grad_send)

    def turn_weights(d):
        blocks = []
        for col in range(3):
            top = w_all[d, KBLOCK * col : KBLOCK * (col + 1), :].astype(jnp.float32)
            begin = LOW + KBLOCK // 2 * col
            low = w_all[d, begin : begin + KBLOCK // 2, :].astype(jnp.float32)
            low = jnp.concatenate([low, pltpu.roll(low, 64, 1)], axis=0)
            blocks.append((top, low))
        top = jnp.transpose(jnp.concatenate([b[0] for b in blocks], axis=0))
        low = jnp.transpose(jnp.concatenate([b[1] for b in blocks], axis=0))
        w_turned[d, :WIDTH, :] = top.astype(jnp.bfloat16)
        w_turned[d, WIDTH:, :] = low[:64].astype(jnp.bfloat16)

    def part_step(p):
        pixels = pl.ds(pl.multiple_of(p * 256, 256), 256)
        total = None
        for d in range(HALF):
            term = jnp.dot(w_turned[d], stack[d, :, pixels], preferred_element_type=jnp.float32)
            total = term if total is None else total + term
        part[2 * p] = total[:, :WIDTH]
        part[2 * p + 1] = total[:, WIDTH:]

    a_send(2)
    for d in (1, 3):
        drain(adj.at[d], a_r.at[d])
        beside_send(d)
    beside_wait(0)
    stack_step(0)
    grad_step(0)
    drain(adj.at[2], a_r.at[2])
    beside_send(2)
    turn_weights(0)
    for d in (1, 3, 2):
        beside_wait(d)
        stack_step(d)
        grad_step(d)
    drain(w_all.at[pl.ds(1, HALF - 1), pl.ds(0, 15 * SHARE)], w_r.at[1])
    loop(1, HALF, turn_weights)
    loop(2 * (1 - k), 2 * (1 - k) + 2, part_step)
    send(part.at[pl.ds(4 * (1 - k), 4)], part_in, part_s, part_r, other)
    loop(2 * k, 2 * k + 2, part_step)

    def red_send(d, chip_z):
        rows = pl.ds(pl.multiple_of(chip_z * PIECE, PIECE), PIECE)
        send(
            red.at[d, rows],
            red_in.at[z_low * HALF + lax.rem(HALF - d, HALF)],
            red_s,
            red_r,
            (r - z_low + chip_z, lax.rem(c + 2 * d, CHAN)),
        )

    def reduce_step(d):
        drain(grad_in.at[d, pl.ds(0, PLANE - 1)], grad_r.at[d])

        def add_step(i, total):
            return total + grad_in[d, i].astype(jnp.float32)

        red[d] = lax.fori_loop(0, PLANE, add_step, jnp.zeros((SHARE, WIDTH), jnp.float32))
        red_send(d, 1 - z_low)
        if d > 0:
            red_send(d, z_low)

    reduce_step(0)
    for d in (1, 3, 2):
        reduce_step(d)
    red_in[z_low * HALF] = red[0, pl.ds(pl.multiple_of(z_low * PIECE, PIECE), PIECE), :]

    mine = [
        x_all[block_of(g) + (pl.ds(pl.multiple_of(k * 96, 32), 96),)].astype(jnp.float32)
        for g in range(CHAN)
    ]
    drain(part_in, part_r)
    results = []
    for f in range(4):
        values = jnp.concatenate([m[GROUP * f : GROUP * f + GROUP] for m in mine], axis=0)
        scale, normed = norm_of(values, gains)
        s = sigmoid(normed)
        adjoint = part[4 * k + f] + part_in[f]
        normed_adjoint = adjoint * s * (1.0 + normed * (1.0 - s)) * gains
        projection = jnp.sum(normed_adjoint * values, axis=0, keepdims=True)
        results.append(
            scale * normed_adjoint - values * (scale * scale * scale * projection / CHANNELS)
        )
    for g in range(CHAN):
        rows = jnp.concatenate([y[GROUP * g : GROUP * g + GROUP] for y in results], axis=0)
        staged[g] = rows.astype(jnp.bfloat16)

    mine_out = pl.ds(pl.multiple_of(c * 96, 32), 96)

    def out_send(d):
        target = lax.rem(c + d, CHAN)
        send(staged.at[target], x_grad.at[mine_out], out_s, out_r, (row, target))

    @pl.when(at_home)
    def _():
        pltpu.make_async_copy(staged.at[c], x_grad.at[mine_out], out_r).start()

    @pl.when(jnp.logical_not(at_home))
    def _():
        out_send(0)

    loop(1, CHAN, out_send)

    drain(red_in.at[pl.ds(0, CHAN - 1)], red_r)
    whole = jnp.zeros((PIECE, WIDTH), jnp.float32)
    for i in range(CHAN):
        whole = whole + red_in[i]
    final[...] = (whole * float(ROWS * ROWS * WIDTH) ** (-0.5)).astype(final.dtype)

    def final_send(d):
        send(final, w_grad.at[r], fin_s, fin_r, {"rows": lax.rem(r + d, ROWS)})

    loop(1, ROWS, final_send)
    own_final = pltpu.make_async_copy(final, w_grad.at[r], local.at[5])
    own_final.start()

    drain(win.at[pl.ds(0, ROWS - 1)], win_s)
    drain(gain_all.at[k, pl.ds(1, HALF - 1)], gain_s)
    drain(x_all.at[k], core_s.at[0])
    drain(gain_all.at[k], core_s.at[1])
    drain(w_all.at[pl.ds(1, HALF - 1), pl.ds(0, SHARE)], w_s.at[0])
    drain(w_all.at[pl.ds(1, HALF - 1), pl.ds(0, 15 * SHARE)], w_s.at[1])
    drain(adj.at[pl.ds(1, HALF - 1)], a_s)

    @pl.when(has_after)
    def _():
        drain(adj, after_s)

    @pl.when(has_before)
    def _():
        drain(adj, before_s)

    drain(grad_in.at[:, pl.ds(0, PLANE - 1)], grad_s)
    drain(part_in, part_s)

    @pl.when(at_home)
    def _():
        drain(x_all.at[k, pl.ds(1, HALF - 1)], x_s)
        drain(staged.at[pl.ds(0, CHAN - 1)], out_s)

    @pl.when(jnp.logical_not(at_home))
    def _():
        drain(x_all.at[k], x_s)
        drain(staged, out_s)

    drain(red_in.at[pl.ds(0, CHAN - 1)], red_s)
    drain(w_grad.at[pl.ds(0, ROWS - 1)], fin_s)
    own_final.wait()
    drain(x_grad, out_r)
    drain(w_grad.at[pl.ds(0, ROWS - 1)], fin_r)


def backward(slot, gain, frames, x, w):
    anywhere = pl.BlockSpec(memory_space=pl.ANY)
    bf16, f32 = jnp.bfloat16, jnp.float32
    one = pltpu.SemaphoreType.DMA
    many = lambda n: pltpu.SemaphoreType.DMA((n,))
    return pl.pallas_call(
        kernel,
        out_shape=(
            jax.ShapeDtypeStruct((ROWS * GROUP, WIDTH), bf16),
            jax.ShapeDtypeStruct((ROWS, PIECE, WIDTH), bf16),
        ),
        in_specs=[anywhere] * 5,
        out_specs=(anywhere, anywhere),
        scratch_shapes=[
            pltpu.SMEM(slot.shape, jnp.int32),
            pltpu.SMEM(gain.shape, f32),
            pltpu.VMEM(frames.shape, bf16),
            pltpu.VMEM(x.shape, bf16),
            pltpu.VMEM(w.shape, bf16),
            pltpu.VMEM((GROUP * ROWS, WIDTH), f32),
            pltpu.SMEM((ROWS,), jnp.int32),
            pltpu.VMEM((ROWS, PADDED, WIDTH), bf16),
            pltpu.VMEM((ROWS, PADDED, WIDTH), bf16),
            pltpu.VMEM((34 * GROUP, WIDTH), bf16),
            pltpu.VMEM((HALF, BLOCK, WIDTH), bf16),
            pltpu.VMEM((2, HALF, BLOCK, WIDTH), bf16),
            pltpu.VMEM((2, HALF, 8 * GROUP, WIDTH), bf16),
            pltpu.VMEM((2, HALF, GROUP, WIDTH), f32),
            pltpu.VMEM((HALF, PACK, WIDTH), bf16),
            pltpu.VMEM((HALF, CHANNELS, LOW), bf16),
            pltpu.VMEM((HALF, LOW, 8 * WIDTH), bf16),
            pltpu.VMEM((8 * WIDTH, CHANNELS), bf16),
            pltpu.VMEM((8, CHANNELS, WIDTH), f32),
            pltpu.VMEM((4, CHANNELS, WIDTH), f32),
            pltpu.VMEM((HALF, PACK, WIDTH), bf16),
            pltpu.VMEM((HALF, PLANE, SHARE, WIDTH), bf16),
            pltpu.VMEM((CHAN, 4 * GROUP, WIDTH), bf16),
            pltpu.VMEM((HALF, SHARE, WIDTH), f32),
            pltpu.VMEM((CHAN, PIECE, WIDTH), f32),
            pltpu.VMEM((PIECE, WIDTH), bf16),
            one, one, one, one, one, one,
            many(2), many(2),
            many(2), many(2),
            one, many(HALF),
            one, one, pltpu.SemaphoreType.DMA((2, HALF)),
            one, many(HALF),
            one, one, one, one, one, one, one, one,
            many(6),
        ],
        compiler_params=pltpu.CompilerParams(
            collective_id=0, has_side_effects=True, vmem_limit_bytes=VMEM_LIMIT
        ),
    )(slot, gain, frames, x, w)


def unpack_kernel(x_in, w_in, x_out, w_out, held_x, held_w, spread, sems):
    x_copy = pltpu.make_async_copy(x_in, held_x, sems.at[0])
    w_copy = pltpu.make_async_copy(w_in, held_w, sems.at[1])
    w_copy.start()
    x_copy.start()
    x_back = pltpu.make_async_copy(held_x, x_out, sems.at[2])
    w_copy.wait()
    backs = []
    for col in range(3):
        low = held_w[LOW + KBLOCK // 2 * col : LOW + KBLOCK // 2 * (col + 1), :]
        low = low.astype(jnp.float32)
        low = jnp.concatenate([low, pltpu.roll(low, 64, 1)], axis=0)
        top = held_w[KBLOCK * col : KBLOCK * (col + 1), :].astype(jnp.float32)
        for tap in range(9):
            begin = GROUP * tap
            spread[col, tap, :, :WIDTH] = top[begin : begin + GROUP]
            spread[col, tap, :, WIDTH:] = low[begin : begin + GROUP, :64]
        back = pltpu.make_async_copy(spread.at[col], w_out.at[:, col], sems.at[3 + col])
        back.start()
        backs.append(back)
        if col == 0:
            x_copy.wait()
            x_back.start()
    x_back.wait()
    for back in backs:
        back.wait()


def unpack(x, w):
    anywhere = pl.BlockSpec(memory_space=pl.ANY)
    return pl.pallas_call(
        unpack_kernel,
        out_shape=(
            jax.ShapeDtypeStruct((ROWS * GROUP, WIDTH), jnp.bfloat16),
            jax.ShapeDtypeStruct((9, 3, GROUP, CHANNELS), jnp.float32),
        ),
        in_specs=[anywhere] * 2,
        out_specs=(anywhere, anywhere),
        scratch_shapes=[
            pltpu.VMEM(x.shape, x.dtype),
            pltpu.VMEM(w.shape, w.dtype),
            pltpu.VMEM((3, 9, GROUP, CHANNELS), jnp.float32),
            pltpu.SemaphoreType.DMA((6,)),
        ],
        compiler_params=pltpu.CompilerParams(vmem_limit_bytes=VMEM_LIMIT),
    )(x, w)


def shards(frame_adjoint, frame_slot, inputs, gain, weight):
    frames = frame_adjoint.reshape(GROUP * ROWS, WIDTH)
    values = inputs.reshape(ROWS * GROUP, WIDTH)
    x_grad, w_grad = backward(frame_slot, gain, frames, values, weight)
    input_adjoint, weight_adjoint = unpack(x_grad, w_grad.reshape(PACK, WIDTH))
    weight_adjoint = weight_adjoint.reshape(TAPS, GROUP, CHANNELS)
    return input_adjoint.reshape(ROWS, GROUP, 1, WIDTH), weight_adjoint


def solution(mesh):
    in_specs = (
        P("rows", "chan", None, None),
        P(),
        P(None, "chan", "rows", None),
        P("chan"),
        P(None, "chan", None),
    )
    out_specs = (P(None, "chan", "rows", None), P(None, "chan", None))
    return jax.shard_map(shards, mesh=mesh, in_specs=in_specs, out_specs=out_specs, check_vma=False)
```

```python
import jax
import jax.numpy as jnp
from jax import lax
from jax.experimental import pallas as pl
from jax.experimental.pallas import tpu as pltpu
from jax.sharding import PartitionSpec as P

CHANNELS = 192
GROUP = 24
WIDTH = 128
ROWS = 32
CHAN = 8
HALF = 4
RING = 4
PLANE = 16
TAPS = 27
PADDED = 32
FRAMES = 10
BLOCK = FRAMES * GROUP
SLAB = 72
KBLOCK = 224
PACK = 1024
LOW = 3 * KBLOCK
PIECE = PACK // ROWS
SLICE = PACK // RING
SHARE = PACK // PLANE
EPSILON = 1e-06
MESH = pl.DeviceIdType.MESH
VMEM_LIMIT = 56 * 1024 * 1024


def owner_of(row):
    return row + lax.rem(row % 8 // 2, 2) * (1 - 2 * lax.rem(row, 2))


def greet_all(r, c):
    barrier = pltpu.get_barrier_semaphore()

    def tell(rows_index, chan_index):
        pl.semaphore_signal(
            barrier, inc=1, device_id=(rows_index, chan_index), device_id_type=MESH
        )

    def chan_step(d):
        chan_index = lax.rem(c + d, CHAN)
        tell(r, chan_index)
        tell(r + 1 - 2 * lax.rem(r, 2), chan_index)

    loop(1, ROWS, lambda d: tell(lax.rem(r + d, ROWS), c))
    loop(1, CHAN, chan_step)
    return barrier, ROWS - 1 + 2 * (CHAN - 1)


def send(src, dst, send_sem, recv_sem, device):
    pltpu.make_async_remote_copy(
        src_ref=src,
        dst_ref=dst,
        send_sem=send_sem,
        recv_sem=recv_sem,
        device_id=device,
        device_id_type=MESH,
    ).start()


def drain(ref, sem):
    pltpu.make_async_copy(ref, ref, sem).wait()


def loop(low, high, step):
    def body(i, carry):
        step(i)
        return carry

    lax.fori_loop(low, high, body, 0)


def norm_of(values, gain):
    squares = jnp.sum(values * values, axis=0, keepdims=True)
    scale = lax.rsqrt(squares / CHANNELS + EPSILON)
    return scale, values * scale * gain


def sigmoid(v):
    return 1.0 / (1.0 + jnp.exp(-v))


def pair_lanes(low):
    return jnp.concatenate([low[: KBLOCK // 2], low[KBLOCK // 2 :]], axis=1)


def kernel(
    slot_in,
    gain_in,
    frames_in,
    x_in,
    w_in,
    x_grad,
    w_grad,
    slot,
    gain,
    frames,
    x,
    w,
    wide,
    inverse,
    win,
    recv,
    ordered,
    adj,
    beside,
    x_all,
    gain_all,
    w_all,
    w_turned,
    stack,
    hidden,
    part,
    part_in,
    grad,
    grad_in,
    staged,
    red,
    red_in,
    final,
    win_s,
    win_r,
    x_s,
    x_r,
    gain_s,
    gain_r,
    core_s,
    core_r,
    w_s,
    w_r,
    a_s,
    a_r,
    after_s,
    before_s,
    beside_r,
    grad_s,
    grad_r,
    part_s,
    part_r,
    out_s,
    out_r,
    red_s,
    red_r,
    fin_s,
    fin_r,
    local,
):
    r = lax.axis_index("rows")
    c = lax.axis_index("chan")
    h = c // 2
    k = lax.rem(c, 2)
    z_low = lax.rem(r, 2)
    place = r // 2
    chip_x = r // 8
    row = owner_of(r)
    at_home = row == r
    other = {"chan": c + 1 - 2 * k}

    fetches = [
        pltpu.make_async_copy(src, dst, local.at[i])
        for i, (src, dst) in enumerate(
            ((frames_in, frames), (w_in, w), (x_in, x), (gain_in, gain), (slot_in, slot))
        )
    ]
    for fetch in fetches:
        fetch.start()
    barrier, greetings = greet_all(r, c)
    fetches[0].wait()

    wide[...] = frames[...].astype(jnp.float32)
    empty = jnp.zeros((PADDED - GROUP, WIDTH), jnp.float32)

    def win_build(i):
        rows = wide[pl.ds(i, GROUP, stride=ROWS), :]
        win[owner_of(i)] = jnp.concatenate([rows, empty], axis=0).astype(jnp.bfloat16)

    loop(0, ROWS, win_build)
    recv[r] = win[r]
    fetches[3].wait()
    gain_all[k, 0] = jnp.concatenate(
        [jnp.full((1, WIDTH), gain[j], jnp.float32) for j in range(GROUP)], axis=0
    )
    ordered[pl.ds(32 * GROUP, 2 * GROUP), :] = jnp.zeros((2 * GROUP, WIDTH), jnp.bfloat16)

    fetches[1].wait()
    for col in range(3):
        rows = [w[9 * a + 3 * b + col].astype(jnp.float32) for a in range(3) for b in range(3)]
        rows = jnp.concatenate(
            rows + [jnp.zeros((KBLOCK - 3 * SLAB, CHANNELS), jnp.float32)], axis=0
        )
        w_all[0, KBLOCK * col : KBLOCK * (col + 1), :] = rows[:, :WIDTH].astype(jnp.bfloat16)
        begin = LOW + KBLOCK // 2 * col
        w_all[0, begin : begin + KBLOCK // 2, :] = pair_lanes(rows[:, WIDTH:]).astype(jnp.bfloat16)
    w_all[0, PACK - 16 :, :] = jnp.zeros((16, WIDTH), jnp.bfloat16)
    fetches[2].wait()
    fetches[4].wait()

    pl.semaphore_wait(barrier, greetings)

    mine_w = pl.ds(pl.multiple_of(SHARE * place, SHARE), SHARE)

    def w_send(d):
        target = lax.rem(c + 2 * d, CHAN)
        send(w_all.at[0, mine_w], w_all.at[HALF - d, mine_w], w_s.at[0], w_r.at[0], {"chan": target})

    def w_spread(e):
        block = w_all.at[pl.ds(1, HALF - 1), mine_w]
        target = lax.rem(place + e, PLANE) * 2 + z_low
        send(block, block, w_s.at[1], w_r.at[1], {"rows": target})

    def win_send(d):
        target = lax.rem(r + d, ROWS)
        send(win.at[target], recv.at[r], win_s, win_r, {"rows": target})

    loop(1, HALF, w_send)
    loop(1, ROWS, win_send)

    def x_send(d):
        target = lax.rem(c + 2 * d, CHAN)
        begin = pl.multiple_of((target // 2) * 192, 64)
        send(
            x.at[pl.ds(begin, 192)],
            x_all.at[k, lax.rem(HALF - d, HALF)],
            x_s,
            x_r,
            (row, target),
        )

    def gain_send(d):
        target = lax.rem(c + 2 * d, CHAN)
        send(gain_all.at[k, 0], gain_all.at[k, HALF - d], gain_s, gain_r, {"chan": target})

    @pl.when(at_home)
    def _():
        begin = pl.multiple_of(h * 192, 64)
        pltpu.make_async_copy(x.at[pl.ds(begin, 192)], x_all.at[k, 0], x_r).start()

    @pl.when(jnp.logical_not(at_home))
    def _():
        x_send(0)

    loop(1, HALF, x_send)
    loop(1, HALF, gain_send)

    def invert(t):
        found = jnp.int32(0)
        for j in range(ROWS):
            found = jnp.where(slot[j] == t, j, found)
        inverse[t] = found

    loop(0, ROWS, invert)
    drain(w_all.at[pl.ds(1, HALF - 1), pl.ds(0, SHARE)], w_r.at[0])
    loop(1, PLANE, w_spread)
    drain(recv.at[pl.ds(0, ROWS - 1)], win_r)

    def order_step(p):
        low = recv[inverse[2 * p]].astype(jnp.float32)[:GROUP]
        high = recv[inverse[2 * p + 1]].astype(jnp.float32)[:GROUP]
        both = jnp.concatenate([low, high], axis=0).astype(jnp.bfloat16)
        ordered[pl.ds(pl.multiple_of(p * 2 * GROUP, 2 * GROUP), 2 * GROUP), :] = both

    loop(0, ROWS // 2, order_step)

    def a_send(d):
        target = lax.rem(c + 2 * d, CHAN)
        start = pl.multiple_of((target // 2) * (8 * GROUP), 64)
        send(
            ordered.at[pl.ds(start, BLOCK)],
            adj.at[HALF - d],
            a_s,
            a_r.at[HALF - d],
            {"chan": target},
        )

    for d in (1, 3):
        a_send(d)
    adj[0] = ordered[pl.ds(pl.multiple_of(h * (8 * GROUP), 64), BLOCK), :]
    has_after = row < ROWS - 1
    has_before = row > 0

    @pl.when(jnp.logical_not(has_after))
    def _():
        beside[0] = jnp.zeros((HALF, BLOCK, WIDTH), jnp.bfloat16)

    @pl.when(jnp.logical_not(has_before))
    def _():
        beside[1] = jnp.zeros((HALF, BLOCK, WIDTH), jnp.bfloat16)

    def beside_send(d):
        @pl.when(has_after)
        def _():
            target = {"rows": owner_of(row + 1)}
            send(adj.at[d], beside.at[1, d], after_s, beside_r.at[1, d], target)

        @pl.when(has_before)
        def _():
            target = {"rows": owner_of(row - 1)}
            send(adj.at[d], beside.at[0, d], before_s, beside_r.at[0, d], target)

    def beside_wait(d):
        @pl.when(has_after)
        def _():
            drain(beside.at[0, d], beside_r.at[0, d])

        @pl.when(has_before)
        def _():
            drain(beside.at[1, d], beside_r.at[1, d])

    beside_send(0)

    drain(x_all.at[k], x_r)
    drain(gain_all.at[k, pl.ds(1, HALF - 1)], gain_r)
    send(x_all.at[k], x_all.at[k], core_s.at[0], core_r.at[0], other)
    send(gain_all.at[k], gain_all.at[k], core_s.at[1], core_r.at[1], other)

    drain(x_all.at[1 - k], core_r.at[0])
    drain(gain_all.at[1 - k], core_r.at[1])

    def block_of(channel_group):
        return channel_group % 2, lax.rem(channel_group // 2 - h + HALF, HALF)

    gains = jnp.concatenate([gain_all[block_of(g)] for g in range(CHAN)], axis=0)
    for f in range(8):
        values = jnp.concatenate(
            [
                x_all[block_of(g)].astype(jnp.float32)[GROUP * f : GROUP * f + GROUP]
                for g in range(CHAN)
            ],
            axis=0,
        )
        _, normed = norm_of(values, gains)
        turned = jnp.transpose(normed * sigmoid(normed))
        hidden[WIDTH * f : WIDTH * (f + 1), :] = turned.astype(jnp.bfloat16)

    lane = lax.broadcasted_iota(jnp.int32, (BLOCK, WIDTH), 1)

    def stack_step(d):
        three = [beside[0, d], adj[d], beside[1, d]]
        three = [v.astype(jnp.float32) for v in three]
        filler = jnp.zeros((KBLOCK - 3 * SLAB, WIDTH), jnp.float32)
        for col in range(3):
            if col == 0:
                moved = [
                    jnp.where(lane == WIDTH - 1, 0.0, pltpu.roll(v, WIDTH - 1, 1)) for v in three
                ]
            elif col == 1:
                moved = three
            else:
                moved = [jnp.where(lane == 0, 0.0, pltpu.roll(v, 1, 1)) for v in three]
            for f in range(8):
                slab = jnp.concatenate(
                    [
                        moved[b][GROUP * (f + 2 - a) : GROUP * (f + 3 - a)]
                        for a in range(3)
                        for b in range(3)
                    ]
                    + [filler],
                    axis=0,
                )
                stack[d, KBLOCK * col : KBLOCK * (col + 1), WIDTH * f : WIDTH * (f + 1)] = (
                    slab.astype(jnp.bfloat16)
                )

    def grad_step(d):
        sums = jnp.dot(stack[d], hidden[...], preferred_element_type=jnp.float32)
        grad[d, :LOW, :] = sums[:, :WIDTH].astype(jnp.bfloat16)
        for col in range(3):
            begin = LOW + KBLOCK // 2 * col
            low = sums[KBLOCK * col : KBLOCK * (col + 1), WIDTH:]
            grad[d, begin : begin + KBLOCK // 2, :] = pair_lanes(low).astype(jnp.bfloat16)
        grad[d, PACK - 16 :, :] = jnp.zeros((16, WIDTH), jnp.bfloat16)
        grad_in[d, place] = grad[d, pl.ds(pl.multiple_of(place * SHARE, SHARE), SHARE), :]

        def grad_send(e):
            target = lax.rem(place + e, PLANE)
            rows = pl.ds(pl.multiple_of(target * SHARE, SHARE), SHARE)
            send(
                grad.at[d, rows],
                grad_in.at[d, place],
                grad_s,
                grad_r.at[d],
                {"rows": target * 2 + z_low},
            )

        loop(1, PLANE, grad_send)

    def turn_weights(d):
        blocks = []
        for col in range(3):
            top = w_all[d, KBLOCK * col : KBLOCK * (col + 1), :].astype(jnp.float32)
            begin = LOW + KBLOCK // 2 * col
            low = w_all[d, begin : begin + KBLOCK // 2, :].astype(jnp.float32)
            low = jnp.concatenate([low, pltpu.roll(low, 64, 1)], axis=0)
            blocks.append((top, low))
        top = jnp.transpose(jnp.concatenate([b[0] for b in blocks], axis=0))
        low = jnp.transpose(jnp.concatenate([b[1] for b in blocks], axis=0))
        w_turned[d, :WIDTH, :] = top.astype(jnp.bfloat16)
        w_turned[d, WIDTH:, :] = low[:64].astype(jnp.bfloat16)

    def part_step(p):
        pixels = pl.ds(pl.multiple_of(p * 256, 256), 256)
        total = None
        for d in range(HALF):
            term = jnp.dot(w_turned[d], stack[d, :, pixels], preferred_element_type=jnp.float32)
            total = term if total is None else total + term
        part[2 * p] = total[:, :WIDTH]
        part[2 * p + 1] = total[:, WIDTH:]

    a_send(2)
    for d in (1, 3):
        drain(adj.at[d], a_r.at[d])
        beside_send(d)
    beside_wait(0)
    stack_step(0)
    grad_step(0)
    drain(adj.at[2], a_r.at[2])
    beside_send(2)
    for d in (1, 3, 2):
        beside_wait(d)
        stack_step(d)
        grad_step(d)
    drain(w_all.at[pl.ds(1, HALF - 1), pl.ds(0, 15 * SHARE)], w_r.at[1])
    loop(0, HALF, turn_weights)
    loop(2 * (1 - k), 2 * (1 - k) + 2, part_step)
    send(part.at[pl.ds(4 * (1 - k), 4)], part_in, part_s, part_r, other)
    loop(2 * k, 2 * k + 2, part_step)

    def red_send(d, chip_z):
        rows = pl.ds(pl.multiple_of(chip_z * PIECE, PIECE), PIECE)
        send(
            red.at[d, rows],
            red_in.at[z_low * HALF + lax.rem(HALF - d, HALF)],
            red_s,
            red_r,
            (r - z_low + chip_z, lax.rem(c + 2 * d, CHAN)),
        )

    def reduce_step(d):
        drain(grad_in.at[d, pl.ds(0, PLANE - 1)], grad_r.at[d])

        def add_step(i, total):
            return total + grad_in[d, i].astype(jnp.float32)

        red[d] = lax.fori_loop(0, PLANE, add_step, jnp.zeros((SHARE, WIDTH), jnp.float32))
        red_send(d, 1 - z_low)
        if d > 0:
            red_send(d, z_low)

    reduce_step(0)
    for d in (1, 3, 2):
        reduce_step(d)
    red_in[z_low * HALF] = red[0, pl.ds(pl.multiple_of(z_low * PIECE, PIECE), PIECE), :]

    mine = [
        x_all[block_of(g) + (pl.ds(pl.multiple_of(k * 96, 32), 96),)].astype(jnp.float32)
        for g in range(CHAN)
    ]
    drain(part_in, part_r)
    results = []
    for f in range(4):
        values = jnp.concatenate([m[GROUP * f : GROUP * f + GROUP] for m in mine], axis=0)
        scale, normed = norm_of(values, gains)
        s = sigmoid(normed)
        adjoint = part[4 * k + f] + part_in[f]
        normed_adjoint = adjoint * s * (1.0 + normed * (1.0 - s)) * gains
        projection = jnp.sum(normed_adjoint * values, axis=0, keepdims=True)
        results.append(
            scale * normed_adjoint - values * (scale * scale * scale * projection / CHANNELS)
        )
    for g in range(CHAN):
        rows = jnp.concatenate([y[GROUP * g : GROUP * g + GROUP] for y in results], axis=0)
        staged[g] = rows.astype(jnp.bfloat16)

    mine_out = pl.ds(pl.multiple_of(c * 96, 32), 96)

    def out_send(d):
        target = lax.rem(c + d, CHAN)
        send(staged.at[target], x_grad.at[mine_out], out_s, out_r, (row, target))

    @pl.when(at_home)
    def _():
        pltpu.make_async_copy(staged.at[c], x_grad.at[mine_out], out_r).start()

    @pl.when(jnp.logical_not(at_home))
    def _():
        out_send(0)

    loop(1, CHAN, out_send)

    drain(red_in.at[pl.ds(0, CHAN - 1)], red_r)
    whole = jnp.zeros((PIECE, WIDTH), jnp.float32)
    for i in range(CHAN):
        whole = whole + red_in[i]
    final[...] = (whole * float(ROWS * ROWS * WIDTH) ** (-0.5)).astype(final.dtype)

    def final_send(d):
        send(final, w_grad.at[r], fin_s, fin_r, {"rows": lax.rem(r + d, ROWS)})

    loop(1, ROWS, final_send)
    own_final = pltpu.make_async_copy(final, w_grad.at[r], local.at[5])
    own_final.start()

    drain(win.at[pl.ds(0, ROWS - 1)], win_s)
    drain(gain_all.at[k, pl.ds(1, HALF - 1)], gain_s)
    drain(x_all.at[k], core_s.at[0])
    drain(gain_all.at[k], core_s.at[1])
    drain(w_all.at[pl.ds(1, HALF - 1), pl.ds(0, SHARE)], w_s.at[0])
    drain(w_all.at[pl.ds(1, HALF - 1), pl.ds(0, 15 * SHARE)], w_s.at[1])
    drain(adj.at[pl.ds(1, HALF - 1)], a_s)

    @pl.when(has_after)
    def _():
        drain(adj, after_s)

    @pl.when(has_before)
    def _():
        drain(adj, before_s)

    drain(grad_in.at[:, pl.ds(0, PLANE - 1)], grad_s)
    drain(part_in, part_s)

    @pl.when(at_home)
    def _():
        drain(x_all.at[k, pl.ds(1, HALF - 1)], x_s)
        drain(staged.at[pl.ds(0, CHAN - 1)], out_s)

    @pl.when(jnp.logical_not(at_home))
    def _():
        drain(x_all.at[k], x_s)
        drain(staged, out_s)

    drain(red_in.at[pl.ds(0, CHAN - 1)], red_s)
    drain(w_grad.at[pl.ds(0, ROWS - 1)], fin_s)
    own_final.wait()
    drain(x_grad, out_r)
    drain(w_grad.at[pl.ds(0, ROWS - 1)], fin_r)


def backward(slot, gain, frames, x, w):
    anywhere = pl.BlockSpec(memory_space=pl.ANY)
    bf16, f32 = jnp.bfloat16, jnp.float32
    one = pltpu.SemaphoreType.DMA
    many = lambda n: pltpu.SemaphoreType.DMA((n,))
    return pl.pallas_call(
        kernel,
        out_shape=(
            jax.ShapeDtypeStruct((ROWS * GROUP, WIDTH), bf16),
            jax.ShapeDtypeStruct((ROWS, PIECE, WIDTH), bf16),
        ),
        in_specs=[anywhere] * 5,
        out_specs=(anywhere, anywhere),
        scratch_shapes=[
            pltpu.SMEM(slot.shape, jnp.int32),
            pltpu.SMEM(gain.shape, f32),
            pltpu.VMEM(frames.shape, bf16),
            pltpu.VMEM(x.shape, bf16),
            pltpu.VMEM(w.shape, bf16),
            pltpu.VMEM((GROUP * ROWS, WIDTH), f32),
            pltpu.SMEM((ROWS,), jnp.int32),
            pltpu.VMEM((ROWS, PADDED, WIDTH), bf16),
            pltpu.VMEM((ROWS, PADDED, WIDTH), bf16),
            pltpu.VMEM((34 * GROUP, WIDTH), bf16),
            pltpu.VMEM((HALF, BLOCK, WIDTH), bf16),
            pltpu.VMEM((2, HALF, BLOCK, WIDTH), bf16),
            pltpu.VMEM((2, HALF, 8 * GROUP, WIDTH), bf16),
            pltpu.VMEM((2, HALF, GROUP, WIDTH), f32),
            pltpu.VMEM((HALF, PACK, WIDTH), bf16),
            pltpu.VMEM((HALF, CHANNELS, LOW), bf16),
            pltpu.VMEM((HALF, LOW, 8 * WIDTH), bf16),
            pltpu.VMEM((8 * WIDTH, CHANNELS), bf16),
            pltpu.VMEM((8, CHANNELS, WIDTH), f32),
            pltpu.VMEM((4, CHANNELS, WIDTH), f32),
            pltpu.VMEM((HALF, PACK, WIDTH), bf16),
            pltpu.VMEM((HALF, PLANE, SHARE, WIDTH), bf16),
            pltpu.VMEM((CHAN, 4 * GROUP, WIDTH), bf16),
            pltpu.VMEM((HALF, SHARE, WIDTH), f32),
            pltpu.VMEM((CHAN, PIECE, WIDTH), f32),
            pltpu.VMEM((PIECE, WIDTH), bf16),
            one, one, one, one, one, one,
            many(2), many(2),
            many(2), many(2),
            one, many(HALF),
            one, one, pltpu.SemaphoreType.DMA((2, HALF)),
            one, many(HALF),
            one, one, one, one, one, one, one, one,
            many(6),
        ],
        compiler_params=pltpu.CompilerParams(
            collective_id=0, has_side_effects=True, vmem_limit_bytes=VMEM_LIMIT
        ),
    )(slot, gain, frames, x, w)


def unpack_kernel(x_in, w_in, x_out, w_out, held_x, held_w, spread, sems):
    x_copy = pltpu.make_async_copy(x_in, held_x, sems.at[0])
    w_copy = pltpu.make_async_copy(w_in, held_w, sems.at[1])
    w_copy.start()
    x_copy.start()
    x_back = pltpu.make_async_copy(held_x, x_out, sems.at[2])
    w_copy.wait()
    backs = []
    for col in range(3):
        low = held_w[LOW + KBLOCK // 2 * col : LOW + KBLOCK // 2 * (col + 1), :]
        low = low.astype(jnp.float32)
        low = jnp.concatenate([low, pltpu.roll(low, 64, 1)], axis=0)
        top = held_w[KBLOCK * col : KBLOCK * (col + 1), :].astype(jnp.float32)
        for tap in range(9):
            begin = GROUP * tap
            spread[col, tap, :, :WIDTH] = top[begin : begin + GROUP]
            spread[col, tap, :, WIDTH:] = low[begin : begin + GROUP, :64]
        back = pltpu.make_async_copy(spread.at[col], w_out.at[:, col], sems.at[3 + col])
        back.start()
        backs.append(back)
        if col == 0:
            x_copy.wait()
            x_back.start()
    x_back.wait()
    for back in backs:
        back.wait()


def unpack(x, w):
    anywhere = pl.BlockSpec(memory_space=pl.ANY)
    return pl.pallas_call(
        unpack_kernel,
        out_shape=(
            jax.ShapeDtypeStruct((ROWS * GROUP, WIDTH), jnp.bfloat16),
            jax.ShapeDtypeStruct((9, 3, GROUP, CHANNELS), jnp.float32),
        ),
        in_specs=[anywhere] * 2,
        out_specs=(anywhere, anywhere),
        scratch_shapes=[
            pltpu.VMEM(x.shape, x.dtype),
            pltpu.VMEM(w.shape, w.dtype),
            pltpu.VMEM((3, 9, GROUP, CHANNELS), jnp.float32),
            pltpu.SemaphoreType.DMA((6,)),
        ],
        compiler_params=pltpu.CompilerParams(vmem_limit_bytes=VMEM_LIMIT),
    )(x, w)


def shards(frame_adjoint, frame_slot, inputs, gain, weight):
    frames = frame_adjoint.reshape(GROUP * ROWS, WIDTH)
    values = inputs.reshape(ROWS * GROUP, WIDTH)
    x_grad, w_grad = backward(frame_slot, gain, frames, values, weight)
    input_adjoint, weight_adjoint = unpack(x_grad, w_grad.reshape(PACK, WIDTH))
    weight_adjoint = weight_adjoint.reshape(TAPS, GROUP, CHANNELS)
    return input_adjoint.reshape(ROWS, GROUP, 1, WIDTH), weight_adjoint


def solution(mesh):
    in_specs = (
        P("rows", "chan", None, None),
        P(),
        P(None, "chan", "rows", None),
        P("chan"),
        P(None, "chan", None),
    )
    out_specs = (P(None, "chan", "rows", None), P(None, "chan", None))
    return jax.shard_map(shards, mesh=mesh, in_specs=in_specs, out_specs=out_specs, check_vma=False)
```

```python
import jax
import jax.numpy as jnp
from jax import lax
from jax.experimental import pallas as pl
from jax.experimental.pallas import tpu as pltpu
from jax.sharding import PartitionSpec as P

CHANNELS = 192
GROUP = 24
WIDTH = 128
ROWS = 32
CHAN = 8
HALF = 4
RING = 4
PLANE = 16
TAPS = 27
PADDED = 32
FRAMES = 10
BLOCK = FRAMES * GROUP
SLAB = 72
KBLOCK = 224
PACK = 1024
LOW = 3 * KBLOCK
PIECE = PACK // ROWS
SLICE = PACK // RING
SHARE = PACK // PLANE
EPSILON = 1e-06
MESH = pl.DeviceIdType.MESH
VMEM_LIMIT = 56 * 1024 * 1024


def owner_of(row):
    return row + lax.rem(row % 8 // 2, 2) * (1 - 2 * lax.rem(row, 2))


def greet_all(r, c):
    barrier = pltpu.get_barrier_semaphore()

    def tell(rows_index, chan_index):
        pl.semaphore_signal(
            barrier, inc=1, device_id=(rows_index, chan_index), device_id_type=MESH
        )

    def chan_step(d):
        chan_index = lax.rem(c + d, CHAN)
        tell(r, chan_index)
        tell(r + 1 - 2 * lax.rem(r, 2), chan_index)

    loop(1, ROWS, lambda d: tell(lax.rem(r + d, ROWS), c))
    loop(1, CHAN, chan_step)
    return barrier, ROWS - 1 + 2 * (CHAN - 1)


def send(src, dst, send_sem, recv_sem, device):
    pltpu.make_async_remote_copy(
        src_ref=src,
        dst_ref=dst,
        send_sem=send_sem,
        recv_sem=recv_sem,
        device_id=device,
        device_id_type=MESH,
    ).start()


def drain(ref, sem):
    pltpu.make_async_copy(ref, ref, sem).wait()


def loop(low, high, step):
    def body(i, carry):
        step(i)
        return carry

    lax.fori_loop(low, high, body, 0)


def norm_of(values, gain):
    squares = jnp.sum(values * values, axis=0, keepdims=True)
    scale = lax.rsqrt(squares / CHANNELS + EPSILON)
    return scale, values * scale * gain


def sigmoid(v):
    return 1.0 / (1.0 + jnp.exp(-v))


def pair_lanes(low):
    return jnp.concatenate([low[: KBLOCK // 2], low[KBLOCK // 2 :]], axis=1)


def kernel(
    slot_in,
    gain_in,
    frames_in,
    x_in,
    w_in,
    x_grad,
    w_grad,
    slot,
    gain,
    frames,
    x,
    w,
    wide,
    inverse,
    win,
    recv,
    ordered,
    adj,
    beside,
    x_all,
    gain_all,
    w_all,
    w_turned,
    stack,
    hidden,
    part,
    part_in,
    grad,
    grad_in,
    staged,
    red,
    red_in,
    final,
    win_s,
    win_r,
    x_s,
    x_r,
    gain_s,
    gain_r,
    core_s,
    core_r,
    w_s,
    w_r,
    a_s,
    a_r,
    after_s,
    before_s,
    beside_r,
    grad_s,
    grad_r,
    part_s,
    part_r,
    out_s,
    out_r,
    red_s,
    red_r,
    fin_s,
    fin_r,
    local,
):
    r = lax.axis_index("rows")
    c = lax.axis_index("chan")
    h = c // 2
    k = lax.rem(c, 2)
    z_low = lax.rem(r, 2)
    place = r // 2
    chip_x = r // 8
    row = owner_of(r)
    at_home = row == r
    other = {"chan": c + 1 - 2 * k}

    fetches = [
        pltpu.make_async_copy(src, dst, local.at[i])
        for i, (src, dst) in enumerate(
            ((frames_in, frames), (w_in, w), (x_in, x), (gain_in, gain), (slot_in, slot))
        )
    ]
    for fetch in fetches:
        fetch.start()
    barrier, greetings = greet_all(r, c)
    fetches[0].wait()

    wide[...] = frames[...].astype(jnp.float32)
    empty = jnp.zeros((PADDED - GROUP, WIDTH), jnp.float32)

    def win_build(i):
        rows = wide[pl.ds(i, GROUP, stride=ROWS), :]
        win[owner_of(i)] = jnp.concatenate([rows, empty], axis=0).astype(jnp.bfloat16)

    loop(0, ROWS, win_build)
    recv[r] = win[r]
    fetches[3].wait()
    gain_all[k, 0] = jnp.concatenate(
        [jnp.full((1, WIDTH), gain[j], jnp.float32) for j in range(GROUP)], axis=0
    )
    ordered[pl.ds(32 * GROUP, 2 * GROUP), :] = jnp.zeros((2 * GROUP, WIDTH), jnp.bfloat16)

    fetches[1].wait()
    for col in range(3):
        rows = [w[9 * a + 3 * b + col].astype(jnp.float32) for a in range(3) for b in range(3)]
        rows = jnp.concatenate(
            rows + [jnp.zeros((KBLOCK - 3 * SLAB, CHANNELS), jnp.float32)], axis=0
        )
        w_all[0, KBLOCK * col : KBLOCK * (col + 1), :] = rows[:, :WIDTH].astype(jnp.bfloat16)
        begin = LOW + KBLOCK // 2 * col
        w_all[0, begin : begin + KBLOCK // 2, :] = pair_lanes(rows[:, WIDTH:]).astype(jnp.bfloat16)
    w_all[0, PACK - 16 :, :] = jnp.zeros((16, WIDTH), jnp.bfloat16)
    fetches[2].wait()
    fetches[4].wait()

    pl.semaphore_wait(barrier, greetings)

    mine_w = pl.ds(pl.multiple_of(SHARE * place, SHARE), SHARE)

    def w_send(d):
        target = lax.rem(c + 2 * d, CHAN)
        send(w_all.at[0, mine_w], w_all.at[HALF - d, mine_w], w_s.at[0], w_r.at[0], {"chan": target})

    def w_spread(e):
        block = w_all.at[pl.ds(1, HALF - 1), mine_w]
        target = lax.rem(place + e, PLANE) * 2 + z_low
        send(block, block, w_s.at[1], w_r.at[1], {"rows": target})

    def win_send(d):
        target = lax.rem(r + d, ROWS)
        send(win.at[target], recv.at[r], win_s, win_r, {"rows": target})

    loop(1, HALF, w_send)
    loop(1, ROWS, win_send)

    def x_send(d):
        target = lax.rem(c + 2 * d, CHAN)
        begin = pl.multiple_of((target // 2) * 192, 64)
        send(
            x.at[pl.ds(begin, 192)],
            x_all.at[k, lax.rem(HALF - d, HALF)],
            x_s,
            x_r,
            (row, target),
        )

    def gain_send(d):
        target = lax.rem(c + 2 * d, CHAN)
        send(gain_all.at[k, 0], gain_all.at[k, HALF - d], gain_s, gain_r, {"chan": target})

    @pl.when(at_home)
    def _():
        begin = pl.multiple_of(h * 192, 64)
        pltpu.make_async_copy(x.at[pl.ds(begin, 192)], x_all.at[k, 0], x_r).start()

    @pl.when(jnp.logical_not(at_home))
    def _():
        x_send(0)

    loop(1, HALF, x_send)
    loop(1, HALF, gain_send)

    def invert(t):
        found = jnp.int32(0)
        for j in range(ROWS):
            found = jnp.where(slot[j] == t, j, found)
        inverse[t] = found

    loop(0, ROWS, invert)
    drain(w_all.at[pl.ds(1, HALF - 1), pl.ds(0, SHARE)], w_r.at[0])
    loop(1, PLANE, w_spread)
    drain(recv.at[pl.ds(0, ROWS - 1)], win_r)

    def order_step(p):
        low = recv[inverse[2 * p]].astype(jnp.float32)[:GROUP]
        high = recv[inverse[2 * p + 1]].astype(jnp.float32)[:GROUP]
        both = jnp.concatenate([low, high], axis=0).astype(jnp.bfloat16)
        ordered[pl.ds(pl.multiple_of(p * 2 * GROUP, 2 * GROUP), 2 * GROUP), :] = both

    loop(0, ROWS // 2, order_step)

    def a_send(d):
        target = lax.rem(c + 2 * d, CHAN)
        start = pl.multiple_of((target // 2) * (8 * GROUP), 64)
        send(
            ordered.at[pl.ds(start, BLOCK)],
            adj.at[HALF - d],
            a_s,
            a_r.at[HALF - d],
            {"chan": target},
        )

    for d in (1, 3):
        a_send(d)
    adj[0] = ordered[pl.ds(pl.multiple_of(h * (8 * GROUP), 64), BLOCK), :]
    has_after = row < ROWS - 1
    has_before = row > 0

    @pl.when(jnp.logical_not(has_after))
    def _():
        beside[0] = jnp.zeros((HALF, BLOCK, WIDTH), jnp.bfloat16)

    @pl.when(jnp.logical_not(has_before))
    def _():
        beside[1] = jnp.zeros((HALF, BLOCK, WIDTH), jnp.bfloat16)

    def beside_send(d):
        @pl.when(has_after)
        def _():
            target = {"rows": owner_of(row + 1)}
            send(adj.at[d], beside.at[1, d], after_s, beside_r.at[1, d], target)

        @pl.when(has_before)
        def _():
            target = {"rows": owner_of(row - 1)}
            send(adj.at[d], beside.at[0, d], before_s, beside_r.at[0, d], target)

    def beside_wait(d):
        @pl.when(has_after)
        def _():
            drain(beside.at[0, d], beside_r.at[0, d])

        @pl.when(has_before)
        def _():
            drain(beside.at[1, d], beside_r.at[1, d])

    beside_send(0)

    drain(gain_all.at[k, pl.ds(1, HALF - 1)], gain_r)
    send(gain_all.at[k], gain_all.at[k], core_s.at[1], core_r.at[1], other)
    drain(x_all.at[k], x_r)
    send(x_all.at[k], x_all.at[k], core_s.at[0], core_r.at[0], other)

    drain(x_all.at[1 - k], core_r.at[0])
    drain(gain_all.at[1 - k], core_r.at[1])

    def block_of(channel_group):
        return channel_group % 2, lax.rem(channel_group // 2 - h + HALF, HALF)

    gains = jnp.concatenate([gain_all[block_of(g)] for g in range(CHAN)], axis=0)
    for f in range(8):
        values = jnp.concatenate(
            [
                x_all[block_of(g)].astype(jnp.float32)[GROUP * f : GROUP * f + GROUP]
                for g in range(CHAN)
            ],
            axis=0,
        )
        _, normed = norm_of(values, gains)
        turned = jnp.transpose(normed * sigmoid(normed))
        hidden[WIDTH * f : WIDTH * (f + 1), :] = turned.astype(jnp.bfloat16)

    lane = lax.broadcasted_iota(jnp.int32, (BLOCK, WIDTH), 1)

    def stack_step(d):
        three = [beside[0, d], adj[d], beside[1, d]]
        three = [v.astype(jnp.float32) for v in three]
        filler = jnp.zeros((KBLOCK - 3 * SLAB, WIDTH), jnp.float32)
        for col in range(3):
            if col == 0:
                moved = [
                    jnp.where(lane == WIDTH - 1, 0.0, pltpu.roll(v, WIDTH - 1, 1)) for v in three
                ]
            elif col == 1:
                moved = three
            else:
                moved = [jnp.where(lane == 0, 0.0, pltpu.roll(v, 1, 1)) for v in three]
            for f in range(8):
                slab = jnp.concatenate(
                    [
                        moved[b][GROUP * (f + 2 - a) : GROUP * (f + 3 - a)]
                        for a in range(3)
                        for b in range(3)
                    ]
                    + [filler],
                    axis=0,
                )
                stack[d, KBLOCK * col : KBLOCK * (col + 1), WIDTH * f : WIDTH * (f + 1)] = (
                    slab.astype(jnp.bfloat16)
                )

    def grad_step(d):
        sums = jnp.dot(stack[d], hidden[...], preferred_element_type=jnp.float32)
        grad[d, :LOW, :] = sums[:, :WIDTH].astype(jnp.bfloat16)
        for col in range(3):
            begin = LOW + KBLOCK // 2 * col
            low = sums[KBLOCK * col : KBLOCK * (col + 1), WIDTH:]
            grad[d, begin : begin + KBLOCK // 2, :] = pair_lanes(low).astype(jnp.bfloat16)
        grad[d, PACK - 16 :, :] = jnp.zeros((16, WIDTH), jnp.bfloat16)
        grad_in[d, place] = grad[d, pl.ds(pl.multiple_of(place * SHARE, SHARE), SHARE), :]

        def grad_send(e):
            target = lax.rem(place + e, PLANE)
            rows = pl.ds(pl.multiple_of(target * SHARE, SHARE), SHARE)
            send(
                grad.at[d, rows],
                grad_in.at[d, place],
                grad_s,
                grad_r.at[d],
                {"rows": target * 2 + z_low},
            )

        loop(1, PLANE, grad_send)

    def turn_weights(d):
        blocks = []
        for col in range(3):
            top = w_all[d, KBLOCK * col : KBLOCK * (col + 1), :].astype(jnp.float32)
            begin = LOW + KBLOCK // 2 * col
            low = w_all[d, begin : begin + KBLOCK // 2, :].astype(jnp.float32)
            low = jnp.concatenate([low, pltpu.roll(low, 64, 1)], axis=0)
            blocks.append((top, low))
        top = jnp.transpose(jnp.concatenate([b[0] for b in blocks], axis=0))
        low = jnp.transpose(jnp.concatenate([b[1] for b in blocks], axis=0))
        w_turned[d, :WIDTH, :] = top.astype(jnp.bfloat16)
        w_turned[d, WIDTH:, :] = low[:64].astype(jnp.bfloat16)

    def part_step(p):
        pixels = pl.ds(pl.multiple_of(p * 256, 256), 256)
        total = None
        for d in range(HALF):
            term = jnp.dot(w_turned[d], stack[d, :, pixels], preferred_element_type=jnp.float32)
            total = term if total is None else total + term
        part[2 * p] = total[:, :WIDTH]
        part[2 * p + 1] = total[:, WIDTH:]

    a_send(2)
    for d in (1, 3):
        drain(adj.at[d], a_r.at[d])
        beside_send(d)
    beside_wait(0)
    stack_step(0)
    grad_step(0)
    drain(adj.at[2], a_r.at[2])
    beside_send(2)
    for d in (1, 3, 2):
        beside_wait(d)
        stack_step(d)
        grad_step(d)
    drain(w_all.at[pl.ds(1, HALF - 1), pl.ds(0, 15 * SHARE)], w_r.at[1])
    loop(0, HALF, turn_weights)
    loop(2 * (1 - k), 2 * (1 - k) + 2, part_step)
    send(part.at[pl.ds(4 * (1 - k), 4)], part_in, part_s, part_r, other)
    loop(2 * k, 2 * k + 2, part_step)

    def red_send(d, chip_z):
        rows = pl.ds(pl.multiple_of(chip_z * PIECE, PIECE), PIECE)
        send(
            red.at[d, rows],
            red_in.at[z_low * HALF + lax.rem(HALF - d, HALF)],
            red_s,
            red_r,
            (r - z_low + chip_z, lax.rem(c + 2 * d, CHAN)),
        )

    def reduce_step(d):
        drain(grad_in.at[d, pl.ds(0, PLANE - 1)], grad_r.at[d])

        def add_step(i, total):
            return total + grad_in[d, i].astype(jnp.float32)

        red[d] = lax.fori_loop(0, PLANE, add_step, jnp.zeros((SHARE, WIDTH), jnp.float32))
        red_send(d, 1 - z_low)
        if d > 0:
            red_send(d, z_low)

    reduce_step(0)
    for d in (1, 3, 2):
        reduce_step(d)
    red_in[z_low * HALF] = red[0, pl.ds(pl.multiple_of(z_low * PIECE, PIECE), PIECE), :]

    mine = [
        x_all[block_of(g) + (pl.ds(pl.multiple_of(k * 96, 32), 96),)].astype(jnp.float32)
        for g in range(CHAN)
    ]
    drain(part_in, part_r)
    results = []
    for f in range(4):
        values = jnp.concatenate([m[GROUP * f : GROUP * f + GROUP] for m in mine], axis=0)
        scale, normed = norm_of(values, gains)
        s = sigmoid(normed)
        adjoint = part[4 * k + f] + part_in[f]
        normed_adjoint = adjoint * s * (1.0 + normed * (1.0 - s)) * gains
        projection = jnp.sum(normed_adjoint * values, axis=0, keepdims=True)
        results.append(
            scale * normed_adjoint - values * (scale * scale * scale * projection / CHANNELS)
        )
    for g in range(CHAN):
        rows = jnp.concatenate([y[GROUP * g : GROUP * g + GROUP] for y in results], axis=0)
        staged[g] = rows.astype(jnp.bfloat16)

    mine_out = pl.ds(pl.multiple_of(c * 96, 32), 96)

    def out_send(d):
        target = lax.rem(c + d, CHAN)
        send(staged.at[target], x_grad.at[mine_out], out_s, out_r, (row, target))

    @pl.when(at_home)
    def _():
        pltpu.make_async_copy(staged.at[c], x_grad.at[mine_out], out_r).start()

    @pl.when(jnp.logical_not(at_home))
    def _():
        out_send(0)

    loop(1, CHAN, out_send)

    drain(red_in.at[pl.ds(0, CHAN - 1)], red_r)
    whole = jnp.zeros((PIECE, WIDTH), jnp.float32)
    for i in range(CHAN):
        whole = whole + red_in[i]
    final[...] = (whole * float(ROWS * ROWS * WIDTH) ** (-0.5)).astype(final.dtype)

    def final_send(d):
        send(final, w_grad.at[r], fin_s, fin_r, {"rows": lax.rem(r + d, ROWS)})

    loop(1, ROWS, final_send)
    own_final = pltpu.make_async_copy(final, w_grad.at[r], local.at[5])
    own_final.start()

    drain(win.at[pl.ds(0, ROWS - 1)], win_s)
    drain(gain_all.at[k, pl.ds(1, HALF - 1)], gain_s)
    drain(x_all.at[k], core_s.at[0])
    drain(gain_all.at[k], core_s.at[1])
    drain(w_all.at[pl.ds(1, HALF - 1), pl.ds(0, SHARE)], w_s.at[0])
    drain(w_all.at[pl.ds(1, HALF - 1), pl.ds(0, 15 * SHARE)], w_s.at[1])
    drain(adj.at[pl.ds(1, HALF - 1)], a_s)

    @pl.when(has_after)
    def _():
        drain(adj, after_s)

    @pl.when(has_before)
    def _():
        drain(adj, before_s)

    drain(grad_in.at[:, pl.ds(0, PLANE - 1)], grad_s)
    drain(part_in, part_s)

    @pl.when(at_home)
    def _():
        drain(x_all.at[k, pl.ds(1, HALF - 1)], x_s)
        drain(staged.at[pl.ds(0, CHAN - 1)], out_s)

    @pl.when(jnp.logical_not(at_home))
    def _():
        drain(x_all.at[k], x_s)
        drain(staged, out_s)

    drain(red_in.at[pl.ds(0, CHAN - 1)], red_s)
    drain(w_grad.at[pl.ds(0, ROWS - 1)], fin_s)
    own_final.wait()
    drain(x_grad, out_r)
    drain(w_grad.at[pl.ds(0, ROWS - 1)], fin_r)


def backward(slot, gain, frames, x, w):
    anywhere = pl.BlockSpec(memory_space=pl.ANY)
    bf16, f32 = jnp.bfloat16, jnp.float32
    one = pltpu.SemaphoreType.DMA
    many = lambda n: pltpu.SemaphoreType.DMA((n,))
    return pl.pallas_call(
        kernel,
        out_shape=(
            jax.ShapeDtypeStruct((ROWS * GROUP, WIDTH), bf16),
            jax.ShapeDtypeStruct((ROWS, PIECE, WIDTH), bf16),
        ),
        in_specs=[anywhere] * 5,
        out_specs=(anywhere, anywhere),
        scratch_shapes=[
            pltpu.SMEM(slot.shape, jnp.int32),
            pltpu.SMEM(gain.shape, f32),
            pltpu.VMEM(frames.shape, bf16),
            pltpu.VMEM(x.shape, bf16),
            pltpu.VMEM(w.shape, bf16),
            pltpu.VMEM((GROUP * ROWS, WIDTH), f32),
            pltpu.SMEM((ROWS,), jnp.int32),
            pltpu.VMEM((ROWS, PADDED, WIDTH), bf16),
            pltpu.VMEM((ROWS, PADDED, WIDTH), bf16),
            pltpu.VMEM((34 * GROUP, WIDTH), bf16),
            pltpu.VMEM((HALF, BLOCK, WIDTH), bf16),
            pltpu.VMEM((2, HALF, BLOCK, WIDTH), bf16),
            pltpu.VMEM((2, HALF, 8 * GROUP, WIDTH), bf16),
            pltpu.VMEM((2, HALF, GROUP, WIDTH), f32),
            pltpu.VMEM((HALF, PACK, WIDTH), bf16),
            pltpu.VMEM((HALF, CHANNELS, LOW), bf16),
            pltpu.VMEM((HALF, LOW, 8 * WIDTH), bf16),
            pltpu.VMEM((8 * WIDTH, CHANNELS), bf16),
            pltpu.VMEM((8, CHANNELS, WIDTH), f32),
            pltpu.VMEM((4, CHANNELS, WIDTH), f32),
            pltpu.VMEM((HALF, PACK, WIDTH), bf16),
            pltpu.VMEM((HALF, PLANE, SHARE, WIDTH), bf16),
            pltpu.VMEM((CHAN, 4 * GROUP, WIDTH), bf16),
            pltpu.VMEM((HALF, SHARE, WIDTH), f32),
            pltpu.VMEM((CHAN, PIECE, WIDTH), f32),
            pltpu.VMEM((PIECE, WIDTH), bf16),
            one, one, one, one, one, one,
            many(2), many(2),
            many(2), many(2),
            one, many(HALF),
            one, one, pltpu.SemaphoreType.DMA((2, HALF)),
            one, many(HALF),
            one, one, one, one, one, one, one, one,
            many(6),
        ],
        compiler_params=pltpu.CompilerParams(
            collective_id=0, has_side_effects=True, vmem_limit_bytes=VMEM_LIMIT
        ),
    )(slot, gain, frames, x, w)


def unpack_kernel(x_in, w_in, x_out, w_out, held_x, held_w, spread, sems):
    x_copy = pltpu.make_async_copy(x_in, held_x, sems.at[0])
    w_copy = pltpu.make_async_copy(w_in, held_w, sems.at[1])
    w_copy.start()
    x_copy.start()
    x_back = pltpu.make_async_copy(held_x, x_out, sems.at[2])
    w_copy.wait()
    backs = []
    for col in range(3):
        low = held_w[LOW + KBLOCK // 2 * col : LOW + KBLOCK // 2 * (col + 1), :]
        low = low.astype(jnp.float32)
        low = jnp.concatenate([low, pltpu.roll(low, 64, 1)], axis=0)
        top = held_w[KBLOCK * col : KBLOCK * (col + 1), :].astype(jnp.float32)
        for tap in range(9):
            begin = GROUP * tap
            spread[col, tap, :, :WIDTH] = top[begin : begin + GROUP]
            spread[col, tap, :, WIDTH:] = low[begin : begin + GROUP, :64]
        back = pltpu.make_async_copy(spread.at[col], w_out.at[:, col], sems.at[3 + col])
        back.start()
        backs.append(back)
        if col == 0:
            x_copy.wait()
            x_back.start()
    x_back.wait()
    for back in backs:
        back.wait()


def unpack(x, w):
    anywhere = pl.BlockSpec(memory_space=pl.ANY)
    return pl.pallas_call(
        unpack_kernel,
        out_shape=(
            jax.ShapeDtypeStruct((ROWS * GROUP, WIDTH), jnp.bfloat16),
            jax.ShapeDtypeStruct((9, 3, GROUP, CHANNELS), jnp.float32),
        ),
        in_specs=[anywhere] * 2,
        out_specs=(anywhere, anywhere),
        scratch_shapes=[
            pltpu.VMEM(x.shape, x.dtype),
            pltpu.VMEM(w.shape, w.dtype),
            pltpu.VMEM((3, 9, GROUP, CHANNELS), jnp.float32),
            pltpu.SemaphoreType.DMA((6,)),
        ],
        compiler_params=pltpu.CompilerParams(vmem_limit_bytes=VMEM_LIMIT),
    )(x, w)


def shards(frame_adjoint, frame_slot, inputs, gain, weight):
    frames = frame_adjoint.reshape(GROUP * ROWS, WIDTH)
    values = inputs.reshape(ROWS * GROUP, WIDTH)
    x_grad, w_grad = backward(frame_slot, gain, frames, values, weight)
    input_adjoint, weight_adjoint = unpack(x_grad, w_grad.reshape(PACK, WIDTH))
    weight_adjoint = weight_adjoint.reshape(TAPS, GROUP, CHANNELS)
    return input_adjoint.reshape(ROWS, GROUP, 1, WIDTH), weight_adjoint


def solution(mesh):
    in_specs = (
        P("rows", "chan", None, None),
        P(),
        P(None, "chan", "rows", None),
        P("chan"),
        P(None, "chan", None),
    )
    out_specs = (P(None, "chan", "rows", None), P(None, "chan", None))
    return jax.shard_map(shards, mesh=mesh, in_specs=in_specs, out_specs=out_specs, check_vma=False)
```
